128 devices in a mesh: gz: 32 (over z, y, core), gx: 4 (over x).
Axes of the slice: x: 4, y: 4, z: 4, core: 2. Of those that a mesh axis runs over, the one named last changes fastest.
Arguments:
- fields: bfloat16 [64, 128, 32, 64], P(None, 'gz', 'gx'), may hold values from -6 to 6
- block_patch: int32 [32, 32], P('gz', 'gx'), may hold values from -1 to 127, as said below
- fine_in: bfloat16 [32, 32, 64, 512], P('gz', 'gx'), may hold values from -6 to 6
- conv_first: bfloat16 [27, 64, 64], replicated, may hold values from -0.15625 to 0.15625
- restrict_weight: bfloat16 [8, 64, 64], replicated, may hold values from -0.25 to 0.25
- coarse_weight: bfloat16 [27, 64, 64], replicated, may hold values from -0.15625 to 0.15625
- prolong_weight: bfloat16 [8, 64, 64], replicated, may hold values from -0.75 to 0.75
- conv_second: bfloat16 [27, 64, 64], replicated, may hold values from -0.15625 to 0.15625
- refine_weight: bfloat16 [27, 64, 64], replicated, may hold values from -0.15625 to 0.15625
Outputs:
- base_out: bfloat16 [64, 128, 32, 64], P(None, 'gz', 'gx')
- fine_out: bfloat16 [32, 32, 64, 512], P('gz', 'gx')
The draws below stay inside these ranges and needn't reach their ends.
Inputs may be any that keep to these rules, and one draw needn't show every extreme that they name: `block_patch`: entry [g, (k * 4 + h) * 2 + s] is -1 for an empty slot or the index py * 16 + px of a patch of slab g whose row py lies in h * 2 to (h + 1) * 2 - 1. The patches named in one slab are distinct. Within each group of 2 slots the live ones come first, and group (g, k, k) has one or more live slots.
All inputs are finite; a program needn't handle non-finite values.
Results may differ from the reference program's by a relative error of at most 0.007.
Values may be sent and summed in bfloat16 or wider, within the bound.
A program may use at most 128 MiB of HBM per device.

```python
import jax
import jax.numpy as jnp
from jax import lax

CH = 64
PATCH = 4
NX = 64
CAP = 2
SLABS = 32
NZ = 128
NY = 32
NPY = 8
NPX = 16
PYD = 2
SLOTS = 32
BLK = 512
N_GX = 4


def draw_block_patch(key, part):
    key = jax.random.fold_in(key, 11)
    per_host = PYD * NPX
    choose_key, count_key = jax.random.split(key)
    keys = jax.random.split(choose_key, SLABS * N_GX)

    def pick(single):
        return jax.random.permutation(single, per_host)[:N_GX * CAP]
    chosen = jax.vmap(pick)(keys).astype(jnp.int32).reshape(SLABS, N_GX, N_GX, CAP)
    hosts = jnp.arange(N_GX, dtype=jnp.int32)
    patch_ids = (chosen + (hosts * per_host)[None, :, None, None]).transpose(0, 2, 1, 3)
    counts = jax.random.randint(count_key, (SLABS, N_GX, N_GX), 0, CAP + 1)
    diagonal = hosts[:, None] == hosts[None, :]
    counts = jnp.where(diagonal[None], jnp.maximum(counts, 1), counts)
    live = jnp.arange(CAP, dtype=jnp.int32)[None, None, None, :] < counts[..., None]
    return jnp.where(live, patch_ids, -1).reshape(SLABS, N_GX * N_GX * CAP).astype(jnp.int32)


def block_levels(stream_key, extent, cuts, low, largest):
    def one(axis_at, shards_of):
        heights = jax.random.uniform(jax.random.fold_in(jax.random.fold_in(stream_key, 6), axis_at), (shards_of,), jnp.float32, low / len(cuts), largest / len(cuts))
        return jnp.repeat(jnp.exp(heights), extent[axis_at] // shards_of).reshape((-1,) + (1,) * (len(extent) - axis_at - 1))

    gain = one(*cuts[0])
    for cut in cuts[1:]:
        gain = gain * one(*cut)
    return gain


def scatter_about(rng, extent, width, limit, cuts=(), kind=jnp.bfloat16):
    values = jax.random.normal(rng, extent, jnp.float32) * width
    if len(cuts) > 0:
        values = block_levels(rng, extent, cuts, -0.22, 0.18) * values
    return jnp.clip(values, min=-limit, max=limit).astype(kind)


def setup_inputs(seed: int = 0) -> dict:
    key_of = jax.random.split(jax.random.key(seed), 10)
    return {
        "fields": scatter_about(key_of[0], (CH, NZ, NY, NX), 1.0, 6.0, ((1, 32), (2, 4))),
        "block_patch": draw_block_patch(jax.random.fold_in(key_of[9], 71), 0),
        "fine_in": scatter_about(key_of[2], (SLABS, SLOTS, CH, BLK), 1.0, 6.0, ((0, 32), (1, 4))),
        "conv_first": scatter_about(key_of[3], (27, CH, CH), (27 * CH) ** -0.5, 0.15625),
        "restrict_weight": scatter_about(key_of[4], (8, CH, CH), (8 * CH) ** -0.5, 0.25),
        "coarse_weight": scatter_about(key_of[5], (27, CH, CH), (27 * CH) ** -0.5, 0.15625),
        "prolong_weight": scatter_about(key_of[6], (8, CH, CH), CH ** -0.5, 0.75),
        "conv_second": scatter_about(key_of[7], (27, CH, CH), (27 * CH) ** -0.5, 0.15625),
        "refine_weight": scatter_about(key_of[8], (27, CH, CH), (27 * CH) ** -0.5, 0.15625),
    }


def pad_grid(field):
    return jnp.pad(field, ((0, 0), (1, 1), (1, 1), (1, 1)))


def conv_grid(padded, weight, depth):
    outputs = weight.shape[1]
    rows = padded.shape[2] - 2
    cols = padded.shape[3] - 2
    taps = weight.astype(jnp.float32)
    count = (padded.shape[1] - 2) // depth

    def one_block(index):
        block = lax.dynamic_slice_in_dim(padded, index * depth, depth + 2, 1).astype(jnp.float32)
        total = jnp.zeros((outputs, depth, rows, cols), jnp.float32)
        for tap in range(27):
            plane = tap // 9
            line = (tap // 3) % 3
            place = tap % 3
            total = total + jnp.einsum("oc,czyx->ozyx", taps[tap], block[:, plane:plane + depth, line:line + rows, place:place + cols])
        return total

    stacked = lax.map(one_block, jnp.arange(count, dtype=jnp.int32))
    return stacked.transpose(1, 0, 2, 3, 4).reshape(outputs, count * depth, rows, cols)


def reference(fields, block_patch, fine_in, conv_first, restrict_weight, coarse_weight, prolong_weight, conv_second, refine_weight):
    active = jax.nn.silu(conv_grid(pad_grid(fields), conv_first, PATCH)).astype(jnp.bfloat16)
    down_map = restrict_weight.astype(jnp.float32).reshape(2, 2, 2, CH, CH)
    split_active = active.astype(jnp.float32).reshape(CH, NZ // 2, 2, NY // 2, 2, NX // 2, 2)
    coarse_in = jnp.einsum("pqroc,czpyqxr->ozyx", down_map, split_active).astype(jnp.bfloat16)
    coarse_out = jax.nn.silu(conv_grid(pad_grid(coarse_in), coarse_weight, PATCH // 2)).astype(jnp.bfloat16)
    up_map = prolong_weight.astype(jnp.float32).reshape(2, 2, 2, CH, CH)
    lifted = jnp.einsum("pqroc,czyx->ozpyqxr", up_map, coarse_out.astype(jnp.float32)).reshape(CH, NZ, NY, NX)
    summed = (active.astype(jnp.float32) + lifted).astype(jnp.bfloat16)
    grid_out = (fields.astype(jnp.float32) + conv_grid(pad_grid(summed), conv_second, PATCH)).astype(jnp.bfloat16)

    active_pad = pad_grid(active)
    span = PATCH + 2
    edge = 2 * PATCH
    taps = refine_weight.astype(jnp.float32)

    def one_slab(index):
        patch_ids = block_patch[index]
        fine = fine_in[index].reshape(SLOTS, CH, edge, edge, edge)
        live = patch_ids >= 0
        clamped = jnp.maximum(patch_ids, 0).astype(jnp.int32)

        def window(patch_id):
            starts = (jnp.int32(0), (index * PATCH).astype(jnp.int32), ((patch_id // NPX) * PATCH).astype(jnp.int32), ((patch_id % NPX) * PATCH).astype(jnp.int32))
            return lax.dynamic_slice(active_pad, starts, (CH, span, span, span))

        ghost = jax.vmap(window)(clamped)
        for axis_number in (2, 3, 4):
            ghost = jnp.repeat(ghost, 2, axis=axis_number)
        ghost = ghost[:, :, 1:-1, 1:-1, 1:-1]
        filled = ghost.at[:, :, 1:-1, 1:-1, 1:-1].set(fine).astype(jnp.float32)
        total = jnp.zeros((SLOTS, CH, edge, edge, edge), jnp.float32)
        for tap in range(27):
            plane = tap // 9
            line = (tap // 3) % 3
            place = tap % 3
            total = total + jnp.einsum("oc,sczyx->sozyx", taps[tap], filled[:, :, plane:plane + edge, line:line + edge, place:place + edge])
        grown = fine.astype(jnp.float32) + total
        result = jnp.where(live[:, None, None, None, None], grown, jnp.float32(0.0)).astype(jnp.bfloat16)
        coarsened = result.astype(jnp.float32).reshape(SLOTS, CH, PATCH, 2, PATCH, 2, PATCH, 2).mean(axis=(3, 5, 7)).astype(jnp.bfloat16)
        return result.reshape(SLOTS, CH, BLK), coarsened

    fine_out, coarsened = lax.map(one_slab, jnp.arange(SLABS, dtype=jnp.int32))
    pieces = grid_out.reshape(CH, SLABS, PATCH, NPY, PATCH, NPX, PATCH).transpose(1, 3, 5, 0, 2, 4, 6).reshape(SLABS, NPY * NPX, CH, PATCH, PATCH, PATCH)
    target = jnp.where(block_patch >= 0, block_patch, NPY * NPX).astype(jnp.int32)
    slab_ids = jnp.broadcast_to(jnp.arange(SLABS, dtype=jnp.int32)[:, None], target.shape)
    pieces = pieces.at[slab_ids, target].set(coarsened, mode="drop")
    base_out = pieces.reshape(SLABS, NPY, NPX, CH, PATCH, PATCH, PATCH).transpose(3, 0, 4, 1, 5, 2, 6).reshape(CH, NZ, NY, NX)
    return base_out, fine_out
```

```python
import functools

import jax
import jax.numpy as jnp
import numpy as np
from jax import lax
from jax.experimental import pallas as pl
from jax.experimental.pallas import tpu as pltpu
from jax.sharding import PartitionSpec as P

BF = jnp.bfloat16
F32 = jnp.float32
MESH = pl.DeviceIdType.MESH
DIRS = [(dz, dy) for dz in (-1, 0, 1) for dy in (-1, 0, 1) if (dz, dy) != (0, 0)]


def split_table():
    cell = np.arange(512)
    row, col = cell // 64, cell % 64
    table = np.zeros((512, 512), np.float32)
    table[cell, ((row % 2) * 2 + col % 2) * 128 + (row // 2) * 32 + col // 2] = 1
    return table


def spread_table():
    table = np.zeros((128, 512), np.float32)
    for q in range(2):
        for r in range(2):
            for k in range(32):
                table[k, (q * 2 + r) * 128 + q * 64 + 2 * k + r] = 1
    return table


def mean_table():
    cell = np.arange(512)
    z, y, x = cell // 64, cell // 8 % 8, cell % 8
    table = np.zeros((512, 128), np.float32)
    table[cell, (z // 2) * 16 + (y // 2) * 4 + x // 2] = 0.125
    return table


def block_table():
    table = np.zeros((5, 256, 1152), np.float32)
    for m in range(5):
        for tap in range(9):
            for a in range(2):
                for b in range(8):
                    for e in range(8):
                        y, x = b + tap // 3 - 1, e + tap % 3 - 1
                        col = tap * 128 + a * 64 + b * 8 + e
                        ghost = (y // 2 + 1) * 6 + x // 2 + 1
                        if m == 4:
                            table[m, a * 128 + (0, 80)[a] + ghost, col] = 1
                        elif 0 <= y < 8 and 0 <= x < 8:
                            table[m, a * 64 + y * 8 + x, col] = 1
                        else:
                            table[m, 128 + 40 * ((m + 1) % 3) + ghost, col] = 1
    return table


def dot(a, b):
    return jnp.dot(a, b, preferred_element_type=F32)


def silu(v):
    return v / (1.0 + jnp.exp(-v))


def lanes_of(shape):
    return lax.broadcasted_iota(jnp.int32, shape, len(shape) - 1)


def splat(flag, shape):
    return jnp.full(shape, jnp.where(flag, 1.0, 0.0).astype(F32), F32)


def pack_taps(raw, packed):
    for dz in range(3):
        packed[dz * 64 : dz * 64 + 64, :] = jnp.concatenate(
            [raw[dz * 9 + t] for t in range(9)], axis=1
        )


def shifted(tile, period):
    lane = lanes_of(tile.shape) % period
    zero = jnp.zeros_like(tile)
    left = jnp.where(lane != 0, pltpu.roll(tile, 1, 1), zero)
    right = jnp.where(lane != period - 1, pltpu.roll(tile, 127, 1), zero)
    return left, tile, right


def stack_rows(tiles, first, last, x_ref):
    low = lanes_of((64, 128)) < 64
    moved = [shifted(t, 64) for t in tiles]
    for dx in range(3):
        swapped = [pltpu.roll(m[dx], 64, 1) for m in moved]
        count = len(tiles)
        between = [
            jnp.where(low, swapped[max(j, 0)], swapped[min(j + 1, count - 1)])
            for j in range(-1, count)
        ]
        for j in range(first, last):
            at = slice((j - first) * 128, (j - first) * 128 + 128)
            x_ref[dx * 64 : dx * 64 + 64, at] = between[j]
            x_ref[192 + dx * 64 : 256 + dx * 64, at] = moved[j][dx]
            x_ref[384 + dx * 64 : 448 + dx * 64, at] = between[j + 1]


def kernel(
    fields,
    patch,
    fine,
    w_first,
    w_restrict,
    w_coarse,
    w_prolong,
    w_second,
    w_refine,
    t_split,
    t_spread,
    t_mean,
    t_block,
    base_out,
    fine_out,
    fields_v,
    cells,
    field_t,
    raw_first,
    raw_restrict,
    raw_coarse,
    raw_prolong,
    raw_second,
    raw_refine,
    split_v,
    spread_v,
    mean_v,
    block_v,
    fine_v,
    fine_o,
    k_first,
    k_restrict,
    k_coarse,
    k_prolong,
    k_second,
    k_refine,
    lists,
    live_v,
    pick,
    place,
    x_v,
    y_v,
    act,
    summed,
    coarse_i,
    coarse_o,
    xc_v,
    u_v,
    win_o,
    win_i,
    xf_v,
    ret_o,
    ret_i,
    load_sem,
    store_sem,
    s_send,
    s_recv,
    c_send,
    c_recv,
    o_send,
    o_recv,
    l_send,
    l_recv,
    w_send,
    w_recv,
    r_send,
    r_recv,
):
    g = lax.axis_index("gz")
    h = lax.axis_index("gx")
    n_g = lax.axis_size("gz")
    n_h = lax.axis_size("gx")

    def near(dz, dy):
        return (lax.rem(g + dz + n_g, n_g), lax.rem(h + dy + n_h, n_h))

    barrier = pltpu.get_barrier_semaphore()
    partners = DIRS + [(0, 2)]
    for dz, dy in partners:
        pl.semaphore_signal(barrier, inc=1, device_id=near(dz, dy), device_id_type=MESH)

    loads = []
    for i, (src, dst) in enumerate(
        [
            (fields, fields_v),
            (w_first, raw_first),
            (w_restrict, raw_restrict),
            (w_coarse, raw_coarse),
            (t_split, split_v),
            (fine, fine_v),
            (w_refine, raw_refine),
            (t_block, block_v),
            (w_prolong, raw_prolong),
            (w_second, raw_second),
            (t_spread, spread_v),
            (t_mean, mean_v),
        ]
    ):
        loads.append(pltpu.make_async_copy(src, dst, load_sem.at[i]))
        loads[-1].start()

    lists[h] = jnp.zeros((8, 128), jnp.int32)
    lists[h, 0:1, 0:8] = patch[...]

    loads[0].wait()
    cells[...] = fields_v[...].astype(F32).reshape(2048, 64)
    for z in range(4):
        for j in range(4):
            pair = [cells[pl.ds(z * 8 + 2 * j + q, 64, stride=32), :] for q in range(2)]
            field_t[2 + z, 1 + j] = jnp.concatenate(pair, axis=1).astype(BF)

    pl.semaphore_wait(barrier, len(partners))

    def span_of(d, own, width, low, high):
        if d == 0:
            return pl.ds(low, own), pl.ds(low, own)
        if d > 0:
            return pl.ds(low + own - width, width), pl.ds(low - width, width)
        return pl.ds(low, width), pl.ds(high, width)

    sends = []
    for i, (dz, dy) in enumerate(DIRS):
        zs, zd = span_of(dz, 4, 2, 2, 6)
        ys, yd = span_of(dy, 4, 1, 1, 5)
        sends.append(
            pltpu.make_async_remote_copy(
                src_ref=field_t.at[zs, ys],
                dst_ref=field_t.at[zd, yd],
                send_sem=s_send.at[i],
                recv_sem=s_recv.at[i],
                device_id=near(dz, dy),
                device_id_type=MESH,
            )
        )
    for copy in sends:
        copy.start()
    list_sends = []
    for d in range(1, 4):
        list_sends.append(
            pltpu.make_async_remote_copy(
                src_ref=lists.at[h],
                dst_ref=lists.at[h],
                send_sem=l_send.at[d - 1],
                recv_sem=l_recv.at[d - 1],
                device_id=near(0, d),
                device_id_type=MESH,
            )
        )
        list_sends[-1].start()

    for copy in loads[1:]:
        copy.wait()
    pack_taps(raw_first, k_first)
    pack_taps(raw_coarse, k_coarse)
    pack_taps(raw_second, k_second)
    pack_taps(raw_refine, k_refine)
    k_restrict[...] = jnp.concatenate([raw_restrict[t] for t in range(8)], axis=1)
    for p in range(2):
        k_prolong[p * 64 : p * 64 + 64, :] = jnp.concatenate(
            [raw_prolong[p * 4 + t] for t in range(4)], axis=1
        )

    for copy in list_sends:
        copy.wait_recv()
    entry = lax.broadcasted_iota(jnp.int32, (8, 128), 1)
    own = patch[...].astype(F32)
    for s in range(8):
        mine = jnp.sum(
            jnp.where(lanes_of((1, 8)) == s, own, 0.0), axis=1, keepdims=True
        )
        live_v[s : s + 1, :] = jnp.where(jnp.broadcast_to(mine, (1, 128)) >= 0.0, 1.0, 0.0)
    lane = lanes_of((1, 128)).astype(F32)
    line = jnp.floor((lane + 0.5) * (1.0 / 6.0))
    place_x = lane - 6.0 * line - 1.0
    source = lax.broadcasted_iota(jnp.int32, (768, 128), 0).astype(F32)
    target = lanes_of((64, 512)).astype(F32)
    inner = (lax.broadcasted_iota(jnp.int32, (64, 1), 0) % 16).astype(F32)
    inner_y = jnp.floor(inner * 0.25)
    inner = inner_y * 64.0 + (inner - 4.0 * inner_y)
    for k in range(4):
        ids = lists[k].astype(F32)
        for s in range(2):
            at = k * 2 + s
            value = jnp.sum(
                jnp.where(entry == h * 2 + s, ids, 0.0), axis=1, keepdims=True
            )[0:1]
            py = jnp.floor(value * (1.0 / 16.0))
            px4 = 4.0 * (value - 16.0 * py)
            top = 256.0 * (py - 2.0 * h.astype(F32))
            col = place_x + px4
            want = jnp.where(
                (lane < 36.0) & (col >= 0.0) & (col < 64.0),
                (line + 1.0) * 64.0 + col + top,
                -1.0,
            )
            pick[:, at * 128 : at * 128 + 128] = jnp.where(source == want, 1.0, 0.0).astype(BF)
            want = jnp.where(value >= 0.0, inner + px4 + top, -1.0)
            place[at * 64 : at * 64 + 64, :] = jnp.where(target == want, 1.0, 0.0).astype(BF)

    for copy in sends:
        copy.wait_recv()

    first_z, last_z = g == 0, g == n_g - 1
    ok_low = splat(h != 0, (64, 128)).astype(BF)
    ok_high = splat(h != n_h - 1, (64, 128)).astype(BF)

    def conv_first_plane(p, carry):
        out = ((p < 2) & first_z) | ((p >= 6) & last_z)
        ok = splat(jnp.logical_not(out), (64, 128)).astype(BF)
        tiles = [field_t[p, t] * ok for t in range(6)]
        tiles[0] = tiles[0] * ok_low
        tiles[5] = tiles[5] * ok_high
        stack_rows(tiles, 0, 6, x_v)
        y_v[p] = dot(k_first[...], x_v[...])
        return carry

    lax.fori_loop(0, 8, conv_first_plane, 0)

    def first_active(q, carry):
        out = ((q == 0) & first_z) | ((q == 5) & last_z)
        for t in range(6):
            at = slice(t * 128, t * 128 + 128)
            total = y_v[q, 0:64, at] + y_v[q + 1, 64:128, at] + y_v[q + 2, 128:192, at]
            ok = jnp.logical_not(out)
            if t == 0:
                ok = ok & (h != 0)
            if t == 5:
                ok = ok & (h != n_h - 1)
            act[pl.ds(q * 64, 64), at] = (silu(total) * splat(ok, (64, 128))).astype(BF)
        return carry

    lax.fori_loop(0, 6, first_active, 0)

    parted = dot(act[64:320, 128:640], split_v[...]).astype(BF)
    gathered = jnp.concatenate(
        [
            jnp.concatenate(
                [
                    parted[(2 * i + p) * 64 : (2 * i + p) * 64 + 64, f * 128 : f * 128 + 128]
                    for p in range(2)
                    for f in range(4)
                ],
                axis=0,
            )
            for i in range(2)
        ],
        axis=1,
    )
    reduced = dot(k_restrict[...], gathered).astype(BF)
    coarse_i[1, 1] = reduced[:, 0:128]
    coarse_i[2, 1] = reduced[:, 128:256]

    def coarse_copies(buffer, send_sem, recv_sem):
        copies = []
        for i, (dz, dy) in enumerate(DIRS):
            zs, zd = span_of(dz, 2, 1, 1, 3)
            copies.append(
                pltpu.make_async_remote_copy(
                    src_ref=buffer.at[zs, pl.ds(1, 1)],
                    dst_ref=buffer.at[zd, pl.ds(1 - dy, 1)],
                    send_sem=send_sem.at[i],
                    recv_sem=recv_sem.at[i],
                    device_id=near(dz, dy),
                    device_id_type=MESH,
                )
            )
        return copies

    in_sends = coarse_copies(coarse_i, c_send, c_recv)
    for copy in in_sends:
        copy.start()

    def block_windows(k, carry):
        at = pl.ds(pl.multiple_of(k * 256, 128), 256)
        found = dot(act[...], pick[:, at])
        for s in range(2):
            parts = [found[q * 64 : q * 64 + 64, s * 128 : s * 128 + 128] for q in range(6)]
            for t in range(2):
                tile = (
                    parts[3 * t]
                    + pltpu.roll(parts[3 * t + 1], 40, 1)
                    + pltpu.roll(parts[3 * t + 2], 80, 1)
                )
                win_o[t, k, s] = tile.astype(BF)
        return carry

    lax.fori_loop(0, 4, block_windows, 0)
    win_sends = []
    for d in range(1, 4):
        peer = near(0, d)
        win_sends.append(
            pltpu.make_async_remote_copy(
                src_ref=win_o.at[:, peer[1]],
                dst_ref=win_i.at[:, h],
                send_sem=w_send.at[d - 1],
                recv_sem=w_recv.at[d - 1],
                device_id=peer,
                device_id_type=MESH,
            )
        )
        win_sends[-1].start()
    for t in range(2):
        for s in range(2):
            win_i[t, h, s] = win_o[t, h, s]

    for copy in in_sends:
        copy.wait_recv()

    def coarse_tiles(buffer, i):
        tiles = [buffer[i, t] for t in range(3)]
        if i in (0, 3):
            ok = splat(jnp.logical_not(first_z if i == 0 else last_z), (64, 128)).astype(BF)
            tiles = [t * ok for t in tiles]
        return [tiles[0] * ok_low, tiles[1], tiles[2] * ok_high]

    quarter = lanes_of((64, 128))
    for i in range(4):
        before, mid, after = coarse_tiles(coarse_i, i)
        up = jnp.where(quarter < 32, pltpu.roll(before, 32, 1), pltpu.roll(mid, 32, 1))
        down = jnp.where(quarter < 96, pltpu.roll(mid, 96, 1), pltpu.roll(after, 96, 1))
        for dy, tile in enumerate((up, mid, down)):
            for dx, moved in enumerate(shifted(tile, 32)):
                tap = dy * 3 + dx
                xc_v[tap * 64 : tap * 64 + 64, i * 128 : i * 128 + 128] = moved
    total = dot(k_coarse[...], xc_v[...])
    for i in range(2):
        value = (
            total[0:64, i * 128 : i * 128 + 128]
            + total[64:128, i * 128 + 128 : i * 128 + 256]
            + total[128:192, i * 128 + 256 : i * 128 + 384]
        )
        coarse_o[1 + i, 1] = silu(value).astype(BF)
    out_sends = coarse_copies(coarse_o, o_send, o_recv)
    for copy in out_sends:
        copy.start()

    for copy in win_sends:
        copy.wait_recv()
    for m in range(5):
        if m < 4:
            left = fine_v[0, :, :, m * 128 : m * 128 + 128].reshape(512, 128)
            right = win_i[(m + 1) // 3].reshape(512, 128)
        else:
            left = win_i[0].reshape(512, 128)
            right = win_i[1].reshape(512, 128)
        spread = dot(jnp.concatenate([left, right], axis=1), block_v[m]).astype(BF)
        for s in range(8):
            for tap in range(9):
                xf_v[s, tap * 64 : tap * 64 + 64, m * 128 : m * 128 + 128] = spread[
                    s * 64 : s * 64 + 64, tap * 128 : tap * 128 + 128
                ]
    low = lanes_of((64, 128)) < 64

    def refine(s, carry):
        total = dot(k_refine[...], xf_v[s])
        alive = live_v[pl.ds(s, 1), :] > 0.5
        behind = [total[0:64, m * 128 : m * 128 + 128] for m in range(5)]
        ahead = [total[128:192, m * 128 : m * 128 + 128] for m in range(5)]
        behind_r = [pltpu.roll(v, 64, 1) for v in behind[:4]]
        ahead_r = [pltpu.roll(v, 64, 1) for v in ahead[:4]]
        for m in range(4):
            at = slice(m * 128, m * 128 + 128)
            value = total[64:128, at]
            value += jnp.where(low, behind_r[m - 1] if m > 0 else behind[4], behind_r[m])
            value += jnp.where(low, ahead_r[m], ahead_r[m + 1] if m < 3 else ahead[4])
            value += fine_v[0, s, :, at].astype(F32)
            value = jnp.where(jnp.broadcast_to(alive, (64, 128)), value, 0.0)
            fine_o[0, s, :, at] = value.astype(BF)
        return carry

    lax.fori_loop(0, 8, refine, 0)
    fine_store = pltpu.make_async_copy(fine_o, fine_out, store_sem.at[0])
    fine_store.start()
    means = dot(fine_o[0].reshape(512, 512), mean_v[...])
    for k in range(4):
        ret_o[k] = (
            means[k * 128 : k * 128 + 64] + pltpu.roll(means[k * 128 + 64 : k * 128 + 128], 64, 1)
        ).astype(BF)
    ret_sends = []
    for d in range(1, 4):
        peer = near(0, d)
        ret_sends.append(
            pltpu.make_async_remote_copy(
                src_ref=ret_o.at[peer[1]],
                dst_ref=ret_i.at[h],
                send_sem=r_send.at[d - 1],
                recv_sem=r_recv.at[d - 1],
                device_id=peer,
                device_id_type=MESH,
            )
        )
        ret_sends[-1].start()
    ret_i[h] = ret_o[h]

    for copy in out_sends:
        copy.wait_recv()
    for i in range(4):
        before, mid, after = coarse_tiles(coarse_o, i)
        rows = [pltpu.roll(before, 32, 1), mid]
        rows += [pltpu.roll(mid, 128 - 32 * j, 1) for j in range(1, 4)]
        rows.append(after)
        spread = dot(jnp.concatenate(rows, axis=0), spread_v[...]).astype(BF)
        for j in range(6):
            for f in range(4):
                u_v[f * 64 : f * 64 + 64, j * 128 : j * 128 + 128] = spread[
                    j * 64 : j * 64 + 64, f * 128 : f * 128 + 128
                ]
        lifted = dot(k_prolong[...], u_v[...])
        for p in range(2):
            q = 2 * i - 1 + p
            if 0 <= q <= 5:
                at = slice(q * 64, q * 64 + 64)
                summed[at, :] = (
                    act[at, :].astype(F32) + lifted[p * 64 : p * 64 + 64, :]
                ).astype(BF)

    def conv_second_plane(q, carry):
        at = pl.ds(pl.multiple_of(q * 64, 64), 64)
        tiles = [summed[at, t * 128 : t * 128 + 128] for t in range(6)]
        stack_rows(tiles, 1, 5, x_v)
        y_v[q, :, 0:512] = dot(k_second[...], x_v[:, 0:512])
        return carry

    lax.fori_loop(0, 6, conv_second_plane, 0)

    for copy in ret_sends:
        copy.wait_recv()
    wide = lanes_of((64, 512)) % 64 // 16
    back = jnp.concatenate([ret_i[k] for k in range(4)], axis=1)
    zero = jnp.zeros_like(back)
    ones = jnp.where(lanes_of((16, 512)) % 64 < 16, 1.0, 0.0).astype(BF)
    stacked = jnp.concatenate([jnp.where(wide == z, back, zero) for z in range(4)] + [ones], axis=0)
    placed = dot(stacked, place[...])
    for z in range(4):
        for j in range(4):
            at = slice(j * 128, j * 128 + 128)
            value = y_v[z, 0:64, at] + y_v[z + 1, 64:128, at] + y_v[z + 2, 128:192, at]
            value += field_t[2 + z, 1 + j].astype(F32)
            covered = jnp.broadcast_to(placed[256:257, at], (64, 128)) > 0.5
            value = jnp.where(covered, placed[z * 64 : z * 64 + 64, at], value)
            cells[pl.ds(z * 8 + 2 * j, 64, stride=32), :] = value[:, 0:64]
            cells[pl.ds(z * 8 + 2 * j + 1, 64, stride=32), :] = value[:, 64:128]
    fields_v[...] = cells[...].reshape(64, 4, 8, 64).astype(BF)
    base_store = pltpu.make_async_copy(fields_v, base_out, store_sem.at[1])
    base_store.start()
    for copy in sends + list_sends + in_sends + win_sends + out_sends + ret_sends:
        copy.wait_send()
    fine_store.wait()
    base_store.wait()


def body(
    fields,
    block_patch,
    fine_in,
    conv_first,
    restrict_weight,
    coarse_weight,
    prolong_weight,
    conv_second,
    refine_weight,
):
    any_spec = pl.BlockSpec(memory_space=pl.ANY)
    vmem_spec = pl.BlockSpec(memory_space=pltpu.VMEM)
    dma = pltpu.SemaphoreType.DMA
    v = pltpu.VMEM
    return pl.pallas_call(
        kernel,
        out_shape=[
            jax.ShapeDtypeStruct(fields.shape, BF),
            jax.ShapeDtypeStruct(fine_in.shape, BF),
        ],
        in_specs=[any_spec, vmem_spec] + [any_spec] * 11,
        out_specs=[any_spec, any_spec],
        scratch_shapes=[
            v((64, 4, 8, 64), BF),
            v((2048, 64), F32),
            v((8, 6, 64, 128), BF),
            v((27, 64, 64), BF),
            v((8, 64, 64), BF),
            v((27, 64, 64), BF),
            v((8, 64, 64), BF),
            v((27, 64, 64), BF),
            v((27, 64, 64), BF),
            v((512, 512), BF),
            v((128, 512), BF),
            v((512, 128), BF),
            v((5, 256, 1152), BF),
            v((1, 8, 64, 512), BF),
            v((1, 8, 64, 512), BF),
            v((192, 576), BF),
            v((64, 512), BF),
            v((192, 576), BF),
            v((128, 256), BF),
            v((192, 576), BF),
            v((192, 576), BF),
            v((4, 8, 128), jnp.int32),
            v((8, 128), F32),
            v((768, 1024), BF),
            v((512, 512), BF),
            v((576, 768), BF),
            v((8, 192, 768), F32),
            v((384, 768), BF),
            v((384, 768), BF),
            v((4, 3, 64, 128), BF),
            v((4, 3, 64, 128), BF),
            v((576, 512), BF),
            v((256, 768), BF),
            v((2, 4, 2, 64, 128), BF),
            v((2, 4, 2, 64, 128), BF),
            v((8, 576, 640), BF),
            v((4, 64, 128), BF),
            v((4, 64, 128), BF),
            dma((12,)),
            dma((2,)),
            dma((8,)),
            dma((8,)),
            dma((8,)),
            dma((8,)),
            dma((8,)),
            dma((8,)),
            dma((3,)),
            dma((3,)),
            dma((3,)),
            dma((3,)),
            dma((3,)),
            dma((3,)),
        ],
        compiler_params=pltpu.CompilerParams(
            collective_id=0, has_side_effects=True, vmem_limit_bytes=52 * 1024 * 1024
        ),
        cost_estimate=pl.CostEstimate(flops=8 * 10**9, bytes_accessed=8 * 10**6, transcendentals=0),
    )(
        fields,
        block_patch,
        fine_in,
        conv_first,
        restrict_weight,
        coarse_weight,
        prolong_weight,
        conv_second,
        refine_weight,
        jnp.asarray(split_table(), BF),
        jnp.asarray(spread_table(), BF),
        jnp.asarray(mean_table(), BF),
        jnp.asarray(block_table(), BF),
    )


def solution(mesh):
    in_specs = (
        P(None, "gz", "gx", None),
        P("gz", "gx"),
        P("gz", "gx", None, None),
        P(),
        P(),
        P(),
        P(),
        P(),
        P(),
    )
    out_specs = (P(None, "gz", "gx", None), P("gz", "gx", None, None))
    return jax.shard_map(body, mesh=mesh, in_specs=in_specs, out_specs=out_specs, check_vma=False)
```

```python
import jax
import jax.numpy as jnp
import numpy as np
from jax import lax
from jax.experimental import pallas as pl
from jax.experimental.pallas import tpu as pltpu
from jax.sharding import PartitionSpec as P

BF = jnp.bfloat16
F32 = jnp.float32
MESH = pl.DeviceIdType.MESH
DIRS = [(dz, dy) for dz in (-1, 0, 1) for dy in (-1, 0, 1) if (dz, dy) != (0, 0)]


def split_table():
    cell = np.arange(512)
    row, col = cell // 64, cell % 64
    table = np.zeros((640, 512), np.float32)
    table[cell + 64, ((row % 2) * 2 + col % 2) * 128 + (row // 2) * 32 + col // 2] = 1
    return table


def spread_table():
    table = np.zeros((128, 512), np.float32)
    for q in range(2):
        for r in range(2):
            for k in range(32):
                table[k, (q * 2 + r) * 128 + (1 - q) * 64 + 2 * k + r] = 1
    return table


def mean_table():
    cell = np.arange(512)
    z, y, x = cell // 64, cell // 8 % 8, cell % 8
    table = np.zeros((512, 128), np.float32)
    table[cell, (z // 2) * 16 + (y // 2) * 4 + x // 2] = 0.125
    return table


def block_table():
    table = np.zeros((5, 256, 1152), np.float32)
    for m in range(5):
        for tap in range(9):
            for a in range(2):
                for b in range(8):
                    for e in range(8):
                        y, x = b + tap // 3 - 1, e + tap % 3 - 1
                        col = tap * 128 + a * 64 + b * 8 + e
                        ghost = (y // 2 + 1) * 6 + x // 2 + 1
                        if m == 4:
                            table[m, a * 128 + (0, 80)[a] + ghost, col] = 1
                        elif 0 <= y < 8 and 0 <= x < 8:
                            table[m, a * 64 + y * 8 + x, col] = 1
                        else:
                            table[m, 128 + 40 * ((m + 1) % 3) + ghost, col] = 1
    return table


def dot(a, b):
    return jnp.dot(a, b, preferred_element_type=F32)


def silu(v):
    return v / (1.0 + jnp.exp(-v))


def lanes_of(shape):
    return lax.broadcasted_iota(jnp.int32, shape, len(shape) - 1)


def splat(flag, shape):
    return jnp.full(shape, jnp.where(flag, 1.0, 0.0).astype(F32), F32)


def pack_taps(raw, packed):
    for dz in range(3):
        packed[dz * 64 : dz * 64 + 64, :] = jnp.concatenate(
            [raw[dz * 9 + t] for t in range(9)], axis=1
        )


def shifted(tile, period):
    lane = lanes_of(tile.shape) % period
    zero = jnp.zeros_like(tile)
    left = jnp.where(lane != 0, pltpu.roll(tile, 1, 1), zero)
    right = jnp.where(lane != period - 1, pltpu.roll(tile, 127, 1), zero)
    return left, tile, right


def stack_rows(tiles, x_ref, start):
    low = lanes_of((64, 128)) < 64
    moved = [shifted(t, 64) for t in tiles]
    for dx in range(3):
        swapped = [pltpu.roll(m[dx], 64, 1) for m in moved]
        for t in range(len(tiles) - 1):
            at = slice(start + t * 128, start + t * 128 + 128)
            x_ref[dx * 64 : dx * 64 + 64, at] = moved[t][dx]
            x_ref[192 + dx * 64 : 256 + dx * 64, at] = jnp.where(low, swapped[t], swapped[t + 1])
            x_ref[384 + dx * 64 : 448 + dx * 64, at] = moved[t + 1][dx]


def kernel(
    fields,
    patch,
    fine,
    w_first,
    w_restrict,
    w_coarse,
    w_prolong,
    w_second,
    w_refine,
    t_split,
    t_spread,
    t_mean,
    t_block,
    base_out,
    fine_out,
    fields_v,
    cells,
    field_t,
    raw_first,
    raw_restrict,
    raw_coarse,
    raw_prolong,
    raw_second,
    raw_refine,
    split_v,
    spread_v,
    mean_v,
    block_v,
    fine_i,
    fine_o,
    k_first,
    k_restrict,
    k_coarse,
    k_prolong,
    k_second,
    k_refine,
    lists,
    live_v,
    pick,
    place,
    x_v,
    y_v,
    act,
    summed,
    coarse_i,
    u_v,
    win,
    xf_v,
    load_sem,
    own_sem,
    store_sem,
    s_send,
    s_recv,
    c_send,
    c_recv,
    l_send,
    l_recv,
    f_send,
    f_recv,
    b_send,
    b_recv,
):
    g = lax.axis_index("gz")
    h = lax.axis_index("gx")
    n_g = lax.axis_size("gz")
    n_h = lax.axis_size("gx")

    def near(dz, dy):
        return (lax.rem(g + dz + n_g, n_g), lax.rem(h + dy + n_h, n_h))

    barrier = pltpu.get_barrier_semaphore()
    partners = DIRS + [(0, 2)]
    for dz, dy in partners:
        pl.semaphore_signal(barrier, inc=1, device_id=near(dz, dy), device_id_type=MESH)

    loads = []
    for i, (src, dst) in enumerate(
        [
            (fields, fields_v),
            (w_first, raw_first),
            (w_restrict, raw_restrict),
            (t_split, split_v),
            (w_refine, raw_refine),
            (t_block, block_v),
            (w_coarse, raw_coarse),
            (w_prolong, raw_prolong),
            (w_second, raw_second),
            (t_spread, spread_v),
            (t_mean, mean_v),
        ]
    ):
        loads.append(pltpu.make_async_copy(src, dst, load_sem.at[i]))
        loads[-1].start()
    own_fine = pltpu.make_async_copy(
        fine.at[0, pl.ds(2 * h, 2)], fine_i.at[h], own_sem.at[0]
    )
    own_fine.start()

    lists[h] = jnp.zeros((8, 128), jnp.int32)
    lists[h, 0:1, 0:8] = patch[...]

    loads[0].wait()
    cells[...] = fields_v[...].astype(F32).reshape(2048, 64)
    for z in range(4):
        for j in range(4):
            pair = [cells[pl.ds(z * 8 + 2 * j + q, 64, stride=32), :] for q in range(2)]
            field_t[2 + z, 1 + j] = jnp.concatenate(pair, axis=1).astype(BF)

    pl.semaphore_wait(barrier, len(partners))

    def span_of(d, own, width, low, high):
        if d == 0:
            return pl.ds(low, own), pl.ds(low, own)
        if d > 0:
            return pl.ds(low + own - width, width), pl.ds(low - width, width)
        return pl.ds(low, width), pl.ds(high, width)

    sends = {}
    for i, (dz, dy) in enumerate(DIRS):
        zs, zd = span_of(dz, 4, 2, 2, 6)
        ys, yd = span_of(dy, 4, 1, 1, 5)
        sends[dz, dy] = pltpu.make_async_remote_copy(
            src_ref=field_t.at[zs, ys],
            dst_ref=field_t.at[zd, yd],
            send_sem=s_send.at[i],
            recv_sem=s_recv.at[i],
            device_id=near(dz, dy),
            device_id_type=MESH,
        )
    order = [(-1, -1), (-1, 1), (1, -1), (1, 1), (0, -1), (0, 1), (-1, 0), (1, 0)]
    for d in order:
        sends[d].start()
    list_sends = []
    fine_sends = []
    for d in (2, 1, 3):
        peer = near(0, d)
        list_sends.append(
            pltpu.make_async_remote_copy(
                src_ref=lists.at[h],
                dst_ref=lists.at[h],
                send_sem=l_send.at[d - 1],
                recv_sem=l_recv.at[d - 1],
                device_id=peer,
                device_id_type=MESH,
            )
        )
        list_sends[-1].start()
    for d in (2, 1, 3):
        peer = near(0, d)
        fine_sends.append(
            pltpu.make_async_remote_copy(
                src_ref=fine.at[0, pl.ds(2 * peer[1], 2)],
                dst_ref=fine_i.at[h],
                send_sem=f_send.at[d - 1],
                recv_sem=f_recv.at[d - 1],
                device_id=peer,
                device_id_type=MESH,
            )
        )
        fine_sends[-1].start()

    first_z, last_z = g == 0, g == n_g - 1
    ok_low = splat(h != 0, (64, 128)).astype(BF)
    ok_high = splat(h != n_h - 1, (64, 128)).astype(BF)
    ok_first = splat(g != 0, (64, 128)).astype(BF)
    ok_last = splat(g != n_g - 1, (64, 128)).astype(BF)

    def field(p, t):
        tile = field_t[p, t]
        if t == 0:
            tile = tile * ok_low
        if t == 5:
            tile = tile * ok_high
        if p < 2:
            tile = tile * ok_first
        if p >= 6:
            tile = tile * ok_last
        return tile

    turn = [0]

    def conv_part(load, weight, runs):
        x_ref = x_v.at[turn[0] % 2]
        turn[0] += 1
        start = 0
        for p, first, last in runs:
            stack_rows([load(p, t) for t in range(first, last + 2)], x_ref, start)
            start += (last + 1 - first) * 128
        total = dot(weight[...], x_ref[:, 0:start])
        start = 0
        for p, first, last in runs:
            size = (last + 1 - first) * 128
            y_v[p, :, first * 128 : first * 128 + size] = total[:, start : start + size]
            start += size

    loads[1].wait()
    pack_taps(raw_first, k_first)
    conv_part(field, k_first, [(2, 1, 3), (3, 1, 3)])
    conv_part(field, k_first, [(4, 1, 3), (5, 1, 3)])

    for copy in loads[2:]:
        copy.wait()
    pack_taps(raw_coarse, k_coarse)
    pack_taps(raw_second, k_second)
    pack_taps(raw_refine, k_refine)
    k_restrict[...] = jnp.concatenate([raw_restrict[t] for t in range(8)], axis=1)
    for p in range(2):
        k_prolong[p * 64 : p * 64 + 64, :] = jnp.concatenate(
            [raw_prolong[p * 4 + t] for t in range(4)], axis=1
        )

    for copy in list_sends:
        copy.wait_recv()
    entry = lax.broadcasted_iota(jnp.int32, (8, 128), 1)
    lane = lanes_of((1, 128)).astype(F32)
    line = jnp.floor((lane + 0.5) * (1.0 / 6.0))
    place_x = lane - 6.0 * line - 1.0
    source = lax.broadcasted_iota(jnp.int32, (640, 128), 0).astype(F32)
    target = lanes_of((64, 512)).astype(F32)
    inner = (lax.broadcasted_iota(jnp.int32, (64, 1), 0) % 16).astype(F32)
    inner_y = jnp.floor(inner * 0.25)
    inner = inner_y * 64.0 + (inner - 4.0 * inner_y)
    for k in range(4):
        ids = lists[k].astype(F32)
        for s in range(2):
            at = k * 2 + s
            value = jnp.sum(
                jnp.where(entry == h * 2 + s, ids, 0.0), axis=1, keepdims=True
            )[0:1]
            py = jnp.floor(value * (1.0 / 16.0))
            px4 = 4.0 * (value - 16.0 * py)
            top = 256.0 * (py - 2.0 * h.astype(F32))
            col = place_x + px4
            want = jnp.where(
                (lane < 36.0) & (col >= 0.0) & (col < 64.0), line * 64.0 + col + top, -1.0
            )
            pick[:, at * 128 : at * 128 + 128] = jnp.where(source == want, 1.0, 0.0).astype(BF)
            want = jnp.where(value >= 0.0, inner + px4 + top, -1.0)
            place[at * 64 : at * 64 + 64, :] = jnp.where(target == want, 1.0, 0.0).astype(BF)
            live_v[k, s : s + 1, :] = jnp.where(
                jnp.broadcast_to(value, (1, 128)) >= 0.0, 1.0, 0.0
            )

    for d in ((0, -1), (0, 1)):
        sends[d].wait_recv()
    conv_part(field, k_first, [(p, t, t) for p in (2, 3, 4, 5) for t in (0, 4)])
    for d in order[:4] + order[6:]:
        sends[d].wait_recv()
    conv_part(field, k_first, [(0, 0, 4), (1, 0, 4)])
    conv_part(field, k_first, [(6, 0, 4), (7, 0, 4)])

    ok_rows = [jnp.ones((64, 128), F32)] * 5
    half = lanes_of((64, 128))
    ok_rows[0] = jnp.where((half < 64) & (h == 0), 0.0, 1.0)
    ok_rows[4] = jnp.where((half >= 64) & (h == n_h - 1), 0.0, 1.0)
    for q in range(6):
        for t in range(5):
            at = slice(t * 128, t * 128 + 128)
            value = silu(y_v[q, 0:64, at] + y_v[q + 1, 64:128, at] + y_v[q + 2, 128:192, at])
            if t in (0, 4):
                value = value * ok_rows[t]
            if q in (0, 5):
                value = value * splat(g != (0 if q == 0 else n_g - 1), (64, 128))
            act[q * 64 : q * 64 + 64, at] = value.astype(BF)

    parted = dot(act[64:320, :], split_v[...]).astype(BF)
    gathered = jnp.concatenate(
        [
            jnp.concatenate(
                [
                    parted[(2 * i + p) * 64 : (2 * i + p) * 64 + 64, f * 128 : f * 128 + 128]
                    for p in range(2)
                    for f in range(4)
                ],
                axis=0,
            )
            for i in range(2)
        ],
        axis=1,
    )
    reduced = dot(k_restrict[...], gathered).astype(BF)
    coarse_i[2, 1] = reduced[:, 0:128]
    coarse_i[3, 1] = reduced[:, 128:256]

    in_sends = []
    for i, (dz, dy) in enumerate(DIRS):
        in_sends.append(
            pltpu.make_async_remote_copy(
                src_ref=coarse_i.at[pl.ds(2, 2), pl.ds(1, 1)],
                dst_ref=coarse_i.at[pl.ds(2 - 2 * dz, 2), pl.ds(1 - dy, 1)],
                send_sem=c_send.at[i],
                recv_sem=c_recv.at[i],
                device_id=near(dz, dy),
                device_id_type=MESH,
            )
        )
    for i in (0, 2, 5, 7, 3, 4, 1, 6):
        in_sends[i].start()

    for k in range(4):
        found = dot(act[...], pick[:, k * 256 : k * 256 + 256])
        for s in range(2):
            parts = [found[q * 64 : q * 64 + 64, s * 128 : s * 128 + 128] for q in range(6)]
            for t in range(2):
                tile = (
                    parts[3 * t]
                    + pltpu.roll(parts[3 * t + 1], 40, 1)
                    + pltpu.roll(parts[3 * t + 2], 80, 1)
                )
                at = (k * 2 + s) * 64
                win[t, at : at + 64, :] = tile.astype(BF)

    own_fine.wait()
    for copy in fine_sends:
        copy.wait_recv()
    for m in range(5):
        if m < 4:
            left = fine_i[:, :, :, m * 128 : m * 128 + 128].reshape(512, 128)
            right = win[(m + 1) // 3]
        else:
            left = win[0]
            right = win[1]
        spread = dot(jnp.concatenate([left, right], axis=1), block_v[m]).astype(BF)
        for s in range(8):
            for tap in range(9):
                xf_v[s, tap * 64 : tap * 64 + 64, m * 128 : m * 128 + 128] = spread[
                    s * 64 : s * 64 + 64, tap * 128 : tap * 128 + 128
                ]

    low = lanes_of((64, 128)) < 64
    back_sends = []
    for s in range(8):
        total = dot(k_refine[...], xf_v[s])
        alive = jnp.broadcast_to(live_v[s // 2, s % 2 : s % 2 + 1, :], (64, 128)) > 0.5
        behind = [total[0:64, m * 128 : m * 128 + 128] for m in range(5)]
        ahead = [total[128:192, m * 128 : m * 128 + 128] for m in range(5)]
        behind_r = [pltpu.roll(v, 64, 1) for v in behind[:4]]
        ahead_r = [pltpu.roll(v, 64, 1) for v in ahead[:4]]
        for m in range(4):
            at = slice(m * 128, m * 128 + 128)
            value = total[64:128, at]
            value += jnp.where(low, behind_r[m - 1] if m > 0 else behind[4], behind_r[m])
            value += jnp.where(low, ahead_r[m], ahead_r[m + 1] if m < 3 else ahead[4])
            value += fine_i[s // 2, s % 2, :, at].astype(F32)
            value = jnp.where(alive, value, 0.0)
            fine_o[s // 2, s % 2, :, at] = value.astype(BF)

    for d in (2, 1, 3):
        peer = near(0, d)
        back_sends.append(
            pltpu.make_async_remote_copy(
                src_ref=fine_o.at[peer[1]],
                dst_ref=fine_out.at[0, pl.ds(2 * h, 2)],
                send_sem=b_send.at[d - 1],
                recv_sem=b_recv.at[d - 1],
                device_id=peer,
                device_id_type=MESH,
            )
        )
        back_sends[-1].start()
    own_store = pltpu.make_async_copy(
        fine_o.at[h], fine_out.at[0, pl.ds(2 * h, 2)], store_sem.at[0]
    )
    own_store.start()
    means = dot(fine_o[...].reshape(512, 512), mean_v[...])
    back = jnp.concatenate(
        [
            (
                means[k * 128 : k * 128 + 64]
                + pltpu.roll(means[k * 128 + 64 : k * 128 + 128], 64, 1)
            ).astype(BF)
            for k in range(4)
        ],
        axis=1,
    )
    wide = lanes_of((64, 512)) % 64 // 16
    zero = jnp.zeros_like(back)
    ones = jnp.where(lanes_of((16, 512)) % 64 < 16, 1.0, 0.0).astype(BF)
    stacked = jnp.concatenate([jnp.where(wide == z, back, zero) for z in range(4)] + [ones], axis=0)
    placed = dot(stacked, place[...])

    for copy in in_sends:
        copy.wait_recv()
    x_ref = x_v.at[turn[0] % 2]
    turn[0] += 1
    for i in range(6):
        before, mid, after = [coarse_i[i, t] for t in range(3)]
        if i < 2:
            before, mid, after = before * ok_first, mid * ok_first, after * ok_first
        if i >= 4:
            before, mid, after = before * ok_last, mid * ok_last, after * ok_last
        before, after = before * ok_low, after * ok_high
        around = [
            jnp.where(half < 64, pltpu.roll(before, 64, 1), pltpu.roll(mid, 64, 1)),
            jnp.where(half < 32, pltpu.roll(before, 32, 1), pltpu.roll(mid, 32, 1)),
            mid,
            jnp.where(half < 96, pltpu.roll(mid, 96, 1), pltpu.roll(after, 96, 1)),
            jnp.where(half < 64, pltpu.roll(mid, 64, 1), pltpu.roll(after, 64, 1)),
        ]
        for a, tile in enumerate(around):
            for dx, moved in enumerate(shifted(tile, 32)):
                for part, dy in ((0, a), (1, a - 2)):
                    if 0 <= dy < 3:
                        at = slice(i * 256 + part * 128, i * 256 + part * 128 + 128)
                        tap = dy * 3 + dx
                        x_ref[tap * 64 : tap * 64 + 64, at] = moved
    total = dot(k_coarse[...], x_ref[...])
    no_row = jnp.where((half < 32) & (h == 0), 0.0, 1.0)
    no_end = jnp.where((half >= 96) & (h == n_h - 1), 0.0, 1.0)
    rows = []
    for i in range(4):
        parts = []
        for part in range(2):
            at = i * 256 + part * 128
            value = silu(
                total[0:64, at : at + 128]
                + total[64:128, at + 256 : at + 384]
                + total[128:192, at + 512 : at + 640]
            )
            value = value * (no_row if part == 0 else no_end)
            if i in (0, 3):
                value = value * splat(g != (0 if i == 0 else n_g - 1), (64, 128))
            parts.append(value.astype(BF))
        rows += [parts[0]] + [pltpu.roll(parts[0], 128 - 32 * j, 1) for j in range(1, 4)]
        rows += [pltpu.roll(parts[1], 128 - 32 * j, 1) for j in range(2, 4)]
    spread = dot(jnp.concatenate(rows, axis=0), spread_v[...]).astype(BF)
    for i in range(4):
        for t in range(5):
            for f in range(4):
                row = (i * 6 + t + 1 - f // 2) * 64
                at = i * 640 + t * 128
                u_v[f * 64 : f * 64 + 64, at : at + 128] = spread[
                    row : row + 64, f * 128 : f * 128 + 128
                ]
    for i in range(4):
        lifted = dot(k_prolong[...], u_v[:, i * 640 : i * 640 + 640])
        for p in range(2):
            q = 2 * i - 1 + p
            if 0 <= q <= 5:
                at = slice(q * 64, q * 64 + 64)
                summed[at, :] = (
                    act[at, :].astype(F32) + lifted[p * 64 : p * 64 + 64, :]
                ).astype(BF)

    def total_in(q, t):
        return summed[q * 64 : q * 64 + 64, t * 128 : t * 128 + 128]

    for q in (0, 2, 4):
        conv_part(total_in, k_second, [(q, 0, 3), (q + 1, 0, 3)])

    for z in range(4):
        for j in range(4):
            at = slice(j * 128, j * 128 + 128)
            value = y_v[z, 0:64, at] + y_v[z + 1, 64:128, at] + y_v[z + 2, 128:192, at]
            value += field_t[2 + z, 1 + j].astype(F32)
            covered = jnp.broadcast_to(placed[256:257, at], (64, 128)) > 0.5
            value = jnp.where(covered, placed[z * 64 : z * 64 + 64, at], value)
            cells[pl.ds(z * 8 + 2 * j, 64, stride=32), :] = value[:, 0:64]
            cells[pl.ds(z * 8 + 2 * j + 1, 64, stride=32), :] = value[:, 64:128]
    fields_v[...] = cells[...].reshape(64, 4, 8, 64).astype(BF)
    base_store = pltpu.make_async_copy(fields_v, base_out, store_sem.at[1])
    base_store.start()
    for copy in back_sends:
        copy.wait_recv()
    for copy in list(sends.values()) + list_sends + fine_sends + in_sends + back_sends:
        copy.wait_send()
    own_store.wait()
    base_store.wait()


def body(
    fields,
    block_patch,
    fine_in,
    conv_first,
    restrict_weight,
    coarse_weight,
    prolong_weight,
    conv_second,
    refine_weight,
):
    any_spec = pl.BlockSpec(memory_space=pl.ANY)
    vmem_spec = pl.BlockSpec(memory_space=pltpu.VMEM)
    dma = pltpu.SemaphoreType.DMA
    v = pltpu.VMEM
    return pl.pallas_call(
        kernel,
        out_shape=[
            jax.ShapeDtypeStruct(fields.shape, BF),
            jax.ShapeDtypeStruct(fine_in.shape, BF),
        ],
        in_specs=[any_spec, vmem_spec] + [any_spec] * 11,
        out_specs=[any_spec, any_spec],
        scratch_shapes=[
            v((64, 4, 8, 64), BF),
            v((2048, 64), F32),
            v((8, 6, 64, 128), BF),
            v((27, 64, 64), BF),
            v((8, 64, 64), BF),
            v((27, 64, 64), BF),
            v((8, 64, 64), BF),
            v((27, 64, 64), BF),
            v((27, 64, 64), BF),
            v((640, 512), BF),
            v((128, 512), BF),
            v((512, 128), BF),
            v((5, 256, 1152), BF),
            v((4, 2, 64, 512), BF),
            v((4, 2, 64, 512), BF),
            v((192, 576), BF),
            v((64, 512), BF),
            v((192, 576), BF),
            v((128, 256), BF),
            v((192, 576), BF),
            v((192, 576), BF),
            v((4, 8, 128), jnp.int32),
            v((4, 8, 128), F32),
            v((640, 1024), BF),
            v((512, 512), BF),
            v((2, 576, 1536), BF),
            v((8, 192, 640), F32),
            v((384, 640), BF),
            v((384, 640), BF),
            v((6, 3, 64, 128), BF),
            v((256, 2560), BF),
            v((2, 512, 128), BF),
            v((8, 576, 640), BF),
            dma((11,)),
            dma((1,)),
            dma((2,)),
            dma((8,)),
            dma((8,)),
            dma((8,)),
            dma((8,)),
            dma((3,)),
            dma((3,)),
            dma((3,)),
            dma((3,)),
            dma((3,)),
            dma((3,)),
        ],
        compiler_params=pltpu.CompilerParams(
            collective_id=0, has_side_effects=True, vmem_limit_bytes=64 * 1024 * 1024
        ),
        cost_estimate=pl.CostEstimate(flops=8 * 10**9, bytes_accessed=8 * 10**6, transcendentals=0),
    )(
        fields,
        block_patch,
        fine_in,
        conv_first,
        restrict_weight,
        coarse_weight,
        prolong_weight,
        conv_second,
        refine_weight,
        jnp.asarray(split_table(), BF),
        jnp.asarray(spread_table(), BF),
        jnp.asarray(mean_table(), BF),
        jnp.asarray(block_table(), BF),
    )


def solution(mesh):
    in_specs = (
        P(None, "gz", "gx", None),
        P("gz", "gx"),
        P("gz", "gx", None, None),
        P(),
        P(),
        P(),
        P(),
        P(),
        P(),
    )
    out_specs = (P(None, "gz", "gx", None), P("gz", "gx", None, None))
    return jax.shard_map(body, mesh=mesh, in_specs=in_specs, out_specs=out_specs, check_vma=False)
```

```python
import jax
import jax.numpy as jnp
import numpy as np
from jax import lax
from jax.experimental import pallas as pl
from jax.experimental.pallas import tpu as pltpu
from jax.sharding import PartitionSpec as P

BF = jnp.bfloat16
F32 = jnp.float32
MESH = pl.DeviceIdType.MESH
DIRS = [(dz, dy) for dz in (-1, 0, 1) for dy in (-1, 0, 1) if (dz, dy) != (0, 0)]


def split_table():
    cell = np.arange(512)
    row, col = cell // 64, cell % 64
    table = np.zeros((640, 512), np.float32)
    table[cell + 64, ((row % 2) * 2 + col % 2) * 128 + (row // 2) * 32 + col // 2] = 1
    return table


def spread_table():
    table = np.zeros((128, 512), np.float32)
    for q in range(2):
        for r in range(2):
            for k in range(32):
                table[k, (q * 2 + r) * 128 + (1 - q) * 64 + 2 * k + r] = 1
    return table


def mean_table():
    cell = np.arange(512)
    z, y, x = cell // 64, cell // 8 % 8, cell % 8
    table = np.zeros((512, 128), np.float32)
    table[cell, (z // 2) * 16 + (y // 2) * 4 + x // 2] = 0.125
    return table


def block_table():
    table = np.zeros((5, 256, 1152), np.float32)
    for m in range(5):
        for tap in range(9):
            for a in range(2):
                for b in range(8):
                    for e in range(8):
                        y, x = b + tap // 3 - 1, e + tap % 3 - 1
                        col = tap * 128 + a * 64 + b * 8 + e
                        ghost = (y // 2 + 1) * 6 + x // 2 + 1
                        if m == 4:
                            table[m, a * 128 + (0, 80)[a] + ghost, col] = 1
                        elif 0 <= y < 8 and 0 <= x < 8:
                            table[m, a * 64 + y * 8 + x, col] = 1
                        else:
                            table[m, 128 + 40 * ((m + 1) % 3) + ghost, col] = 1
    return table


def dot(a, b):
    return jnp.dot(a, b, preferred_element_type=F32)


def silu(v):
    return v / (1.0 + jnp.exp(-v))


def lanes_of(shape):
    return lax.broadcasted_iota(jnp.int32, shape, len(shape) - 1)


def splat(flag, shape):
    return jnp.full(shape, jnp.where(flag, 1.0, 0.0).astype(F32), F32)


def pack_taps(raw, packed):
    for dz in range(3):
        packed[dz * 64 : dz * 64 + 64, :] = jnp.concatenate(
            [raw[dz * 9 + t] for t in range(9)], axis=1
        )


def shifted(tile, period):
    lane = lanes_of(tile.shape) % period
    zero = jnp.zeros_like(tile)
    left = jnp.where(lane != 0, pltpu.roll(tile, 1, 1), zero)
    right = jnp.where(lane != period - 1, pltpu.roll(tile, 127, 1), zero)
    return left, tile, right


def stack_rows(tiles, x_ref, start):
    low = lanes_of((64, 128)) < 64
    moved = [shifted(t, 64) for t in tiles]
    for dx in range(3):
        swapped = [pltpu.roll(m[dx], 64, 1) for m in moved]
        for t in range(len(tiles) - 1):
            at = slice(start + t * 128, start + t * 128 + 128)
            x_ref[dx * 64 : dx * 64 + 64, at] = moved[t][dx]
            x_ref[192 + dx * 64 : 256 + dx * 64, at] = jnp.where(low, swapped[t], swapped[t + 1])
            x_ref[384 + dx * 64 : 448 + dx * 64, at] = moved[t + 1][dx]


def kernel(
    fields,
    patch,
    fine,
    w_first,
    w_restrict,
    w_coarse,
    w_prolong,
    w_second,
    w_refine,
    t_split,
    t_spread,
    t_mean,
    t_block,
    base_out,
    fine_out,
    fields_v,
    cells,
    field_t,
    raw_first,
    raw_restrict,
    raw_coarse,
    raw_prolong,
    raw_second,
    raw_refine,
    split_v,
    spread_v,
    mean_v,
    block_v,
    fine_i,
    fine_o,
    k_first,
    k_restrict,
    k_coarse,
    k_prolong,
    k_second,
    k_refine,
    lists,
    live_v,
    pick,
    place,
    x_v,
    y_v,
    act,
    summed,
    coarse_i,
    u_v,
    win,
    xf_v,
    load_sem,
    own_sem,
    store_sem,
    s_send,
    s_recv,
    c_send,
    c_recv,
    l_send,
    l_recv,
    f_send,
    f_recv,
    b_send,
    b_recv,
):
    g = lax.axis_index("gz")
    h = lax.axis_index("gx")
    n_g = lax.axis_size("gz")
    n_h = lax.axis_size("gx")

    def near(dz, dy):
        return (lax.rem(g + dz + n_g, n_g), lax.rem(h + dy + n_h, n_h))

    barrier = pltpu.get_barrier_semaphore()
    partners = DIRS + [(0, 2)]
    for dz, dy in partners:
        pl.semaphore_signal(barrier, inc=1, device_id=near(dz, dy), device_id_type=MESH)

    loads = []
    for i, (src, dst) in enumerate(
        [
            (fields, fields_v),
            (w_first, raw_first),
            (w_restrict, raw_restrict),
            (t_split, split_v),
            (w_refine, raw_refine),
            (t_block, block_v),
            (w_coarse, raw_coarse),
            (w_prolong, raw_prolong),
            (w_second, raw_second),
            (t_spread, spread_v),
            (t_mean, mean_v),
        ]
    ):
        loads.append(pltpu.make_async_copy(src, dst, load_sem.at[i]))
    loads[0].start()
    own_fine = pltpu.make_async_copy(
        fine.at[0, pl.ds(2 * h, 2)], fine_i.at[h], own_sem.at[0]
    )

    lists[h] = jnp.zeros((8, 128), jnp.int32)
    lists[h, 0:1, 0:8] = patch[...]

    loads[0].wait()
    for copy in loads[1:] + [own_fine]:
        copy.start()
    cells[...] = fields_v[...].astype(F32).reshape(2048, 64)
    for z in range(4):
        for j in range(4):
            pair = [cells[pl.ds(z * 8 + 2 * j + q, 64, stride=32), :] for q in range(2)]
            field_t[2 + z, 1 + j] = jnp.concatenate(pair, axis=1).astype(BF)

    pl.semaphore_wait(barrier, len(partners))

    def span_of(d, own, width, low, high):
        if d == 0:
            return pl.ds(low, own), pl.ds(low, own)
        if d > 0:
            return pl.ds(low + own - width, width), pl.ds(low - width, width)
        return pl.ds(low, width), pl.ds(high, width)

    sends = {}
    for i, (dz, dy) in enumerate(DIRS):
        zs, zd = span_of(dz, 4, 2, 2, 6)
        ys, yd = span_of(dy, 4, 1, 1, 5)
        sends[dz, dy] = pltpu.make_async_remote_copy(
            src_ref=field_t.at[zs, ys],
            dst_ref=field_t.at[zd, yd],
            send_sem=s_send.at[i],
            recv_sem=s_recv.at[i],
            device_id=near(dz, dy),
            device_id_type=MESH,
        )
    order = [(-1, -1), (-1, 1), (1, -1), (1, 1), (0, -1), (0, 1), (-1, 0), (1, 0)]
    for d in order:
        sends[d].start()
    list_sends = []
    fine_sends = []
    for d in (2, 1, 3):
        peer = near(0, d)
        list_sends.append(
            pltpu.make_async_remote_copy(
                src_ref=lists.at[h],
                dst_ref=lists.at[h],
                send_sem=l_send.at[d - 1],
                recv_sem=l_recv.at[d - 1],
                device_id=peer,
                device_id_type=MESH,
            )
        )
        list_sends[-1].start()
    first_z, last_z = g == 0, g == n_g - 1
    ok_low = splat(h != 0, (64, 128)).astype(BF)
    ok_high = splat(h != n_h - 1, (64, 128)).astype(BF)
    ok_first = splat(g != 0, (64, 128)).astype(BF)
    ok_last = splat(g != n_g - 1, (64, 128)).astype(BF)

    def field(p, t):
        tile = field_t[p, t]
        if t == 0:
            tile = tile * ok_low
        if t == 5:
            tile = tile * ok_high
        if p < 2:
            tile = tile * ok_first
        if p >= 6:
            tile = tile * ok_last
        return tile

    turn = [0]

    def conv_part(load, weight, runs):
        x_ref = x_v.at[turn[0] % 2]
        turn[0] += 1
        start = 0
        for p, first, last in runs:
            stack_rows([load(p, t) for t in range(first, last + 2)], x_ref, start)
            start += (last + 1 - first) * 128
        total = dot(weight[...], x_ref[:, 0:start])
        start = 0
        for p, first, last in runs:
            size = (last + 1 - first) * 128
            y_v[p, :, first * 128 : first * 128 + size] = total[:, start : start + size]
            start += size

    loads[1].wait()
    pack_taps(raw_first, k_first)
    conv_part(field, k_first, [(2, 1, 3), (3, 1, 3)])
    conv_part(field, k_first, [(4, 1, 3), (5, 1, 3)])

    for d in order:
        sends[d].wait_send()
    for d in (2, 1, 3):
        peer = near(0, d)
        fine_sends.append(
            pltpu.make_async_remote_copy(
                src_ref=fine.at[0, pl.ds(2 * peer[1], 2)],
                dst_ref=fine_i.at[h],
                send_sem=f_send.at[d - 1],
                recv_sem=f_recv.at[d - 1],
                device_id=peer,
                device_id_type=MESH,
            )
        )
        fine_sends[-1].start()


    for copy in loads[2:]:
        copy.wait()
    pack_taps(raw_coarse, k_coarse)
    pack_taps(raw_second, k_second)
    pack_taps(raw_refine, k_refine)
    k_restrict[...] = jnp.concatenate([raw_restrict[t] for t in range(8)], axis=1)
    for p in range(2):
        k_prolong[p * 64 : p * 64 + 64, :] = jnp.concatenate(
            [raw_prolong[p * 4 + t] for t in range(4)], axis=1
        )

    for copy in list_sends:
        copy.wait_recv()
    entry = lax.broadcasted_iota(jnp.int32, (8, 128), 1)
    lane = lanes_of((1, 128)).astype(F32)
    line = jnp.floor((lane + 0.5) * (1.0 / 6.0))
    place_x = lane - 6.0 * line - 1.0
    source = lax.broadcasted_iota(jnp.int32, (640, 128), 0).astype(F32)
    target = lanes_of((64, 512)).astype(F32)
    inner = (lax.broadcasted_iota(jnp.int32, (64, 1), 0) % 16).astype(F32)
    inner_y = jnp.floor(inner * 0.25)
    inner = inner_y * 64.0 + (inner - 4.0 * inner_y)
    for k in range(4):
        ids = lists[k].astype(F32)
        for s in range(2):
            at = k * 2 + s
            value = jnp.sum(
                jnp.where(entry == h * 2 + s, ids, 0.0), axis=1, keepdims=True
            )[0:1]
            py = jnp.floor(value * (1.0 / 16.0))
            px4 = 4.0 * (value - 16.0 * py)
            top = 256.0 * (py - 2.0 * h.astype(F32))
            col = place_x + px4
            want = jnp.where(
                (lane < 36.0) & (col >= 0.0) & (col < 64.0), line * 64.0 + col + top, -1.0
            )
            pick[:, at * 128 : at * 128 + 128] = jnp.where(source == want, 1.0, 0.0).astype(BF)
            want = jnp.where(value >= 0.0, inner + px4 + top, -1.0)
            place[at * 64 : at * 64 + 64, :] = jnp.where(target == want, 1.0, 0.0).astype(BF)
            live_v[k, s : s + 1, :] = jnp.where(
                jnp.broadcast_to(value, (1, 128)) >= 0.0, 1.0, 0.0
            )

    for d in ((0, -1), (0, 1)):
        sends[d].wait_recv()
    conv_part(field, k_first, [(p, t, t) for p in (2, 3, 4, 5) for t in (0, 4)])
    for d in order[:4] + order[6:]:
        sends[d].wait_recv()
    conv_part(field, k_first, [(0, 0, 4), (1, 0, 4)])
    conv_part(field, k_first, [(6, 0, 4), (7, 0, 4)])

    ok_rows = [jnp.ones((64, 128), F32)] * 5
    half = lanes_of((64, 128))
    ok_rows[0] = jnp.where((half < 64) & (h == 0), 0.0, 1.0)
    ok_rows[4] = jnp.where((half >= 64) & (h == n_h - 1), 0.0, 1.0)
    for q in range(6):
        for t in range(5):
            at = slice(t * 128, t * 128 + 128)
            value = silu(y_v[q, 0:64, at] + y_v[q + 1, 64:128, at] + y_v[q + 2, 128:192, at])
            if t in (0, 4):
                value = value * ok_rows[t]
            if q in (0, 5):
                value = value * splat(g != (0 if q == 0 else n_g - 1), (64, 128))
            act[q * 64 : q * 64 + 64, at] = value.astype(BF)

    parted = dot(act[64:320, :], split_v[...]).astype(BF)
    gathered = jnp.concatenate(
        [
            jnp.concatenate(
                [
                    parted[(2 * i + p) * 64 : (2 * i + p) * 64 + 64, f * 128 : f * 128 + 128]
                    for p in range(2)
                    for f in range(4)
                ],
                axis=0,
            )
            for i in range(2)
        ],
        axis=1,
    )
    reduced = dot(k_restrict[...], gathered).astype(BF)
    coarse_i[2, 1] = reduced[:, 0:128]
    coarse_i[3, 1] = reduced[:, 128:256]

    in_sends = []
    for i, (dz, dy) in enumerate(DIRS):
        in_sends.append(
            pltpu.make_async_remote_copy(
                src_ref=coarse_i.at[pl.ds(2, 2), pl.ds(1, 1)],
                dst_ref=coarse_i.at[pl.ds(2 - 2 * dz, 2), pl.ds(1 - dy, 1)],
                send_sem=c_send.at[i],
                recv_sem=c_recv.at[i],
                device_id=near(dz, dy),
                device_id_type=MESH,
            )
        )
    for i in (0, 2, 5, 7, 3, 4, 1, 6):
        in_sends[i].start()

    for k in range(4):
        found = dot(act[...], pick[:, k * 256 : k * 256 + 256])
        for s in range(2):
            parts = [found[q * 64 : q * 64 + 64, s * 128 : s * 128 + 128] for q in range(6)]
            for t in range(2):
                tile = (
                    parts[3 * t]
                    + pltpu.roll(parts[3 * t + 1], 40, 1)
                    + pltpu.roll(parts[3 * t + 2], 80, 1)
                )
                at = (k * 2 + s) * 64
                win[t, at : at + 64, :] = tile.astype(BF)

    own_fine.wait()
    for copy in fine_sends:
        copy.wait_recv()
    for m in range(5):
        if m < 4:
            left = fine_i[:, :, :, m * 128 : m * 128 + 128].reshape(512, 128)
            right = win[(m + 1) // 3]
        else:
            left = win[0]
            right = win[1]
        spread = dot(jnp.concatenate([left, right], axis=1), block_v[m]).astype(BF)
        for s in range(8):
            for tap in range(9):
                xf_v[s, tap * 64 : tap * 64 + 64, m * 128 : m * 128 + 128] = spread[
                    s * 64 : s * 64 + 64, tap * 128 : tap * 128 + 128
                ]

    low = lanes_of((64, 128)) < 64
    back_sends = []
    for d in (2, 1, 3, 0):
        peer = near(0, d)
        k = peer[1]
        for s in range(2):
            total = dot(k_refine[...], xf_v[k * 2 + s])
            alive = jnp.broadcast_to(live_v[k, s : s + 1, :], (64, 128)) > 0.5
            behind = [total[0:64, m * 128 : m * 128 + 128] for m in range(5)]
            ahead = [total[128:192, m * 128 : m * 128 + 128] for m in range(5)]
            behind_r = [pltpu.roll(v, 64, 1) for v in behind[:4]]
            ahead_r = [pltpu.roll(v, 64, 1) for v in ahead[:4]]
            for m in range(4):
                at = slice(m * 128, m * 128 + 128)
                value = total[64:128, at]
                value += jnp.where(low, behind_r[m - 1] if m > 0 else behind[4], behind_r[m])
                value += jnp.where(low, ahead_r[m], ahead_r[m + 1] if m < 3 else ahead[4])
                value += fine_i[k, s, :, at].astype(F32)
                value = jnp.where(alive, value, 0.0)
                fine_o[k, s, :, at] = value.astype(BF)
        if d == 0:
            continue
        back_sends.append(
            pltpu.make_async_remote_copy(
                src_ref=fine_o.at[k],
                dst_ref=fine_out.at[0, pl.ds(2 * h, 2)],
                send_sem=b_send.at[d - 1],
                recv_sem=b_recv.at[d - 1],
                device_id=peer,
                device_id_type=MESH,
            )
        )
        back_sends[-1].start()
    own_store = pltpu.make_async_copy(
        fine_o.at[h], fine_out.at[0, pl.ds(2 * h, 2)], store_sem.at[0]
    )
    own_store.start()
    means = dot(fine_o[...].reshape(512, 512), mean_v[...])
    back = jnp.concatenate(
        [
            (
                means[k * 128 : k * 128 + 64]
                + pltpu.roll(means[k * 128 + 64 : k * 128 + 128], 64, 1)
            ).astype(BF)
            for k in range(4)
        ],
        axis=1,
    )
    wide = lanes_of((64, 512)) % 64 // 16
    zero = jnp.zeros_like(back)
    ones = jnp.where(lanes_of((16, 512)) % 64 < 16, 1.0, 0.0).astype(BF)
    stacked = jnp.concatenate([jnp.where(wide == z, back, zero) for z in range(4)] + [ones], axis=0)
    placed = dot(stacked, place[...])

    for copy in in_sends:
        copy.wait_recv()
    x_ref = x_v.at[turn[0] % 2]
    turn[0] += 1
    for i in range(6):
        before, mid, after = [coarse_i[i, t] for t in range(3)]
        if i < 2:
            before, mid, after = before * ok_first, mid * ok_first, after * ok_first
        if i >= 4:
            before, mid, after = before * ok_last, mid * ok_last, after * ok_last
        before, after = before * ok_low, after * ok_high
        around = [
            jnp.where(half < 64, pltpu.roll(before, 64, 1), pltpu.roll(mid, 64, 1)),
            jnp.where(half < 32, pltpu.roll(before, 32, 1), pltpu.roll(mid, 32, 1)),
            mid,
            jnp.where(half < 96, pltpu.roll(mid, 96, 1), pltpu.roll(after, 96, 1)),
            jnp.where(half < 64, pltpu.roll(mid, 64, 1), pltpu.roll(after, 64, 1)),
        ]
        for a, tile in enumerate(around):
            for dx, moved in enumerate(shifted(tile, 32)):
                for part, dy in ((0, a), (1, a - 2)):
                    if 0 <= dy < 3:
                        at = slice(i * 256 + part * 128, i * 256 + part * 128 + 128)
                        tap = dy * 3 + dx
                        x_ref[tap * 64 : tap * 64 + 64, at] = moved
    total = dot(k_coarse[...], x_ref[...])
    no_row = jnp.where((half < 32) & (h == 0), 0.0, 1.0)
    no_end = jnp.where((half >= 96) & (h == n_h - 1), 0.0, 1.0)
    rows = []
    for i in range(4):
        parts = []
        for part in range(2):
            at = i * 256 + part * 128
            value = silu(
                total[0:64, at : at + 128]
                + total[64:128, at + 256 : at + 384]
                + total[128:192, at + 512 : at + 640]
            )
            value = value * (no_row if part == 0 else no_end)
            if i in (0, 3):
                value = value * splat(g != (0 if i == 0 else n_g - 1), (64, 128))
            parts.append(value.astype(BF))
        rows += [parts[0]] + [pltpu.roll(parts[0], 128 - 32 * j, 1) for j in range(1, 4)]
        rows += [pltpu.roll(parts[1], 128 - 32 * j, 1) for j in range(2, 4)]
    spread = dot(jnp.concatenate(rows, axis=0), spread_v[...]).astype(BF)
    for i in range(4):
        for t in range(5):
            for f in range(4):
                row = (i * 6 + t + 1 - f // 2) * 64
                at = i * 640 + t * 128
                u_v[f * 64 : f * 64 + 64, at : at + 128] = spread[
                    row : row + 64, f * 128 : f * 128 + 128
                ]
    for i in range(4):
        lifted = dot(k_prolong[...], u_v[:, i * 640 : i * 640 + 640])
        for p in range(2):
            q = 2 * i - 1 + p
            if 0 <= q <= 5:
                at = slice(q * 64, q * 64 + 64)
                summed[at, :] = (
                    act[at, :].astype(F32) + lifted[p * 64 : p * 64 + 64, :]
                ).astype(BF)

    def total_in(q, t):
        return summed[q * 64 : q * 64 + 64, t * 128 : t * 128 + 128]

    for q in (0, 2, 4):
        conv_part(total_in, k_second, [(q, 0, 3), (q + 1, 0, 3)])

    for z in range(4):
        for j in range(4):
            at = slice(j * 128, j * 128 + 128)
            value = y_v[z, 0:64, at] + y_v[z + 1, 64:128, at] + y_v[z + 2, 128:192, at]
            value += field_t[2 + z, 1 + j].astype(F32)
            covered = jnp.broadcast_to(placed[256:257, at], (64, 128)) > 0.5
            value = jnp.where(covered, placed[z * 64 : z * 64 + 64, at], value)
            cells[pl.ds(z * 8 + 2 * j, 64, stride=32), :] = value[:, 0:64]
            cells[pl.ds(z * 8 + 2 * j + 1, 64, stride=32), :] = value[:, 64:128]
    fields_v[...] = cells[...].reshape(64, 4, 8, 64).astype(BF)
    base_store = pltpu.make_async_copy(fields_v, base_out, store_sem.at[1])
    base_store.start()
    for copy in back_sends:
        copy.wait_recv()
    for copy in list_sends + fine_sends + in_sends + back_sends:
        copy.wait_send()
    own_store.wait()
    base_store.wait()


def finish(base, fine, base_out, fine_out, base_v, fine_v, in_sems, out_sems):
    loads = []
    stores = []
    for i in range(4):
        parts = [
            (base, base_v, base_out, (pl.ds(16 * i, 16),)),
            (fine, fine_v, fine_out, (pl.ds(0, 1), pl.ds(2 * i, 2))),
        ]
        for j, (src, mid, dst, at) in enumerate(parts):
            loads.append(pltpu.make_async_copy(src.at[at], mid.at[at], in_sems.at[2 * i + j]))
            stores.append(pltpu.make_async_copy(mid.at[at], dst.at[at], out_sems.at[2 * i + j]))
    for copy in loads:
        copy.start()
    for load, store in zip(loads, stores):
        load.wait()
        store.start()
    for copy in stores:
        copy.wait()


def body(
    fields,
    block_patch,
    fine_in,
    conv_first,
    restrict_weight,
    coarse_weight,
    prolong_weight,
    conv_second,
    refine_weight,
):
    any_spec = pl.BlockSpec(memory_space=pl.ANY)
    vmem_spec = pl.BlockSpec(memory_space=pltpu.VMEM)
    dma = pltpu.SemaphoreType.DMA
    v = pltpu.VMEM
    results = pl.pallas_call(
        kernel,
        out_shape=[
            jax.ShapeDtypeStruct(fields.shape, BF),
            jax.ShapeDtypeStruct(fine_in.shape, BF),
        ],
        in_specs=[any_spec, vmem_spec] + [any_spec] * 11,
        out_specs=[any_spec, any_spec],
        scratch_shapes=[
            v((64, 4, 8, 64), BF),
            v((2048, 64), F32),
            v((8, 6, 64, 128), BF),
            v((27, 64, 64), BF),
            v((8, 64, 64), BF),
            v((27, 64, 64), BF),
            v((8, 64, 64), BF),
            v((27, 64, 64), BF),
            v((27, 64, 64), BF),
            v((640, 512), BF),
            v((128, 512), BF),
            v((512, 128), BF),
            v((5, 256, 1152), BF),
            v((4, 2, 64, 512), BF),
            v((4, 2, 64, 512), BF),
            v((192, 576), BF),
            v((64, 512), BF),
            v((192, 576), BF),
            v((128, 256), BF),
            v((192, 576), BF),
            v((192, 576), BF),
            v((4, 8, 128), jnp.int32),
            v((4, 8, 128), F32),
            v((640, 1024), BF),
            v((512, 512), BF),
            v((2, 576, 1536), BF),
            v((8, 192, 640), F32),
            v((384, 640), BF),
            v((384, 640), BF),
            v((6, 3, 64, 128), BF),
            v((256, 2560), BF),
            v((2, 512, 128), BF),
            v((8, 576, 640), BF),
            dma((11,)),
            dma((1,)),
            dma((2,)),
            dma((8,)),
            dma((8,)),
            dma((8,)),
            dma((8,)),
            dma((3,)),
            dma((3,)),
            dma((3,)),
            dma((3,)),
            dma((3,)),
            dma((3,)),
        ],
        compiler_params=pltpu.CompilerParams(
            collective_id=0, has_side_effects=True, vmem_limit_bytes=64 * 1024 * 1024
        ),
        cost_estimate=pl.CostEstimate(flops=8 * 10**9, bytes_accessed=8 * 10**6, transcendentals=0),
    )(
        fields,
        block_patch,
        fine_in,
        conv_first,
        restrict_weight,
        coarse_weight,
        prolong_weight,
        conv_second,
        refine_weight,
        jnp.asarray(split_table(), BF),
        jnp.asarray(spread_table(), BF),
        jnp.asarray(mean_table(), BF),
        jnp.asarray(block_table(), BF),
    )
    return pl.pallas_call(
        finish,
        out_shape=[
            jax.ShapeDtypeStruct(fields.shape, BF),
            jax.ShapeDtypeStruct(fine_in.shape, BF),
        ],
        in_specs=[any_spec, any_spec],
        out_specs=[any_spec, any_spec],
        scratch_shapes=[
            v(fields.shape, BF),
            v(fine_in.shape, BF),
            dma((8,)),
            dma((8,)),
        ],
        compiler_params=pltpu.CompilerParams(vmem_limit_bytes=64 * 1024 * 1024),
    )(*results)


def solution(mesh):
    in_specs = (
        P(None, "gz", "gx", None),
        P("gz", "gx"),
        P("gz", "gx", None, None),
        P(),
        P(),
        P(),
        P(),
        P(),
        P(),
    )
    out_specs = (P(None, "gz", "gx", None), P("gz", "gx", None, None))
    return jax.shard_map(body, mesh=mesh, in_specs=in_specs, out_specs=out_specs, check_vma=False)
```

```python
import jax
import jax.numpy as jnp
import numpy as np
from jax import lax
from jax.experimental import pallas as pl
from jax.experimental.pallas import tpu as pltpu
from jax.sharding import PartitionSpec as P

BF = jnp.bfloat16
F32 = jnp.float32
MESH = pl.DeviceIdType.MESH
DIRS = [(dz, dy) for dz in (-1, 0, 1) for dy in (-1, 0, 1) if (dz, dy) != (0, 0)]


def split_table():
    cell = np.arange(512)
    row, col = cell // 64, cell % 64
    table = np.zeros((640, 512), np.float32)
    table[cell + 64, ((row % 2) * 2 + col % 2) * 128 + (row // 2) * 32 + col // 2] = 1
    return table


def spread_table():
    table = np.zeros((128, 512), np.float32)
    for q in range(2):
        for r in range(2):
            for k in range(32):
                table[k, (q * 2 + r) * 128 + (1 - q) * 64 + 2 * k + r] = 1
    return table


def mean_table():
    cell = np.arange(512)
    z, y, x = cell // 64, cell // 8 % 8, cell % 8
    table = np.zeros((512, 128), np.float32)
    table[cell, (z // 2) * 16 + (y // 2) * 4 + x // 2] = 0.125
    return table


def block_table():
    table = np.zeros((5, 256, 1152), np.float32)
    for m in range(5):
        for tap in range(9):
            for a in range(2):
                for b in range(8):
                    for e in range(8):
                        y, x = b + tap // 3 - 1, e + tap % 3 - 1
                        col = tap * 128 + a * 64 + b * 8 + e
                        ghost = (y // 2 + 1) * 6 + x // 2 + 1
                        if m == 4:
                            table[m, a * 128 + (0, 80)[a] + ghost, col] = 1
                        elif 0 <= y < 8 and 0 <= x < 8:
                            table[m, a * 64 + y * 8 + x, col] = 1
                        else:
                            table[m, 128 + 40 * ((m + 1) % 3) + ghost, col] = 1
    return table


def dot(a, b):
    return jnp.dot(a, b, preferred_element_type=F32)


def silu(v):
    return v / (1.0 + jnp.exp(-v))


def lanes_of(shape):
    return lax.broadcasted_iota(jnp.int32, shape, len(shape) - 1)


def splat(flag, shape):
    return jnp.full(shape, jnp.where(flag, 1.0, 0.0).astype(F32), F32)


def pack_taps(raw, packed):
    for dz in range(3):
        packed[dz * 64 : dz * 64 + 64, :] = jnp.concatenate(
            [raw[dz * 9 + t] for t in range(9)], axis=1
        )


def shifted(tile, period):
    lane = lanes_of(tile.shape) % period
    zero = jnp.zeros_like(tile)
    left = jnp.where(lane != 0, pltpu.roll(tile, 1, 1), zero)
    right = jnp.where(lane != period - 1, pltpu.roll(tile, 127, 1), zero)
    return left, tile, right


def stack_rows(tiles, x_ref, start):
    low = lanes_of((64, 128)) < 64
    moved = [shifted(t, 64) for t in tiles]
    for dx in range(3):
        swapped = [pltpu.roll(m[dx], 64, 1) for m in moved]
        for t in range(len(tiles) - 1):
            at = slice(start + t * 128, start + t * 128 + 128)
            x_ref[dx * 64 : dx * 64 + 64, at] = moved[t][dx]
            x_ref[192 + dx * 64 : 256 + dx * 64, at] = jnp.where(low, swapped[t], swapped[t + 1])
            x_ref[384 + dx * 64 : 448 + dx * 64, at] = moved[t + 1][dx]


def kernel(
    fields,
    patch,
    fine,
    w_first,
    w_restrict,
    w_coarse,
    w_prolong,
    w_second,
    w_refine,
    t_split,
    t_spread,
    t_mean,
    t_block,
    base_out,
    fine_out,
    fields_v,
    cells,
    field_t,
    raw_first,
    raw_restrict,
    raw_coarse,
    raw_prolong,
    raw_second,
    raw_refine,
    split_v,
    spread_v,
    mean_v,
    block_v,
    fine_i,
    fine_o,
    k_first,
    k_restrict,
    k_coarse,
    k_prolong,
    k_second,
    k_refine,
    lists,
    live_v,
    pick,
    place,
    x_v,
    y_v,
    act,
    summed,
    coarse_i,
    edge_o,
    edge_i,
    u_v,
    win,
    xf_v,
    load_sem,
    own_sem,
    store_sem,
    s_send,
    s_recv,
    c_send,
    c_recv,
    l_send,
    l_recv,
    f_send,
    f_recv,
    b_send,
    b_recv,
):
    g = lax.axis_index("gz")
    h = lax.axis_index("gx")
    n_g = lax.axis_size("gz")
    n_h = lax.axis_size("gx")

    def near(dz, dy):
        return (lax.rem(g + dz + n_g, n_g), lax.rem(h + dy + n_h, n_h))

    barrier = pltpu.get_barrier_semaphore()
    partners = DIRS + [(0, 2)]
    for dz, dy in partners:
        pl.semaphore_signal(barrier, inc=1, device_id=near(dz, dy), device_id_type=MESH)

    loads = []
    for i, (src, dst) in enumerate(
        [
            (fields, fields_v),
            (w_first, raw_first),
            (w_restrict, raw_restrict),
            (t_split, split_v),
            (w_refine, raw_refine),
            (t_block, block_v),
            (w_coarse, raw_coarse),
            (w_prolong, raw_prolong),
            (w_second, raw_second),
            (t_spread, spread_v),
            (t_mean, mean_v),
        ]
    ):
        loads.append(pltpu.make_async_copy(src, dst, load_sem.at[i]))
    loads[0].start()
    own_fine = pltpu.make_async_copy(
        fine.at[0, pl.ds(2 * h, 2)], fine_i.at[h], own_sem.at[0]
    )

    lists[h] = jnp.zeros((8, 128), jnp.int32)
    lists[h, 0:1, 0:8] = patch[...]

    loads[0].wait()
    for copy in loads[1:] + [own_fine]:
        copy.start()
    cells[...] = fields_v[...].astype(F32).reshape(2048, 64)
    for z in range(4):
        for j in range(4):
            pair = [cells[pl.ds(z * 8 + 2 * j + q, 64, stride=32), :] for q in range(2)]
            field_t[2 + z, 1 + j] = jnp.concatenate(pair, axis=1).astype(BF)

    pl.semaphore_wait(barrier, len(partners))

    def span_of(d, own, width, low, high):
        if d == 0:
            return pl.ds(low, own), pl.ds(low, own)
        if d > 0:
            return pl.ds(low + own - width, width), pl.ds(low - width, width)
        return pl.ds(low, width), pl.ds(high, width)

    sends = {}
    for i, (dz, dy) in enumerate(DIRS):
        zs, zd = span_of(dz, 4, 2, 2, 6)
        ys, yd = span_of(dy, 4, 1, 1, 5)
        sends[dz, dy] = pltpu.make_async_remote_copy(
            src_ref=field_t.at[zs, ys],
            dst_ref=field_t.at[zd, yd],
            send_sem=s_send.at[i],
            recv_sem=s_recv.at[i],
            device_id=near(dz, dy),
            device_id_type=MESH,
        )
    order = [(-1, -1), (-1, 1), (1, -1), (1, 1), (0, -1), (0, 1), (-1, 0), (1, 0)]
    for d in order:
        sends[d].start()
    list_sends = []
    fine_sends = []
    for d in (2, 1, 3):
        peer = near(0, d)
        list_sends.append(
            pltpu.make_async_remote_copy(
                src_ref=lists.at[h],
                dst_ref=lists.at[h],
                send_sem=l_send.at[d - 1],
                recv_sem=l_recv.at[d - 1],
                device_id=peer,
                device_id_type=MESH,
            )
        )
        list_sends[-1].start()
    first_z, last_z = g == 0, g == n_g - 1
    ok_low = splat(h != 0, (64, 128)).astype(BF)
    ok_high = splat(h != n_h - 1, (64, 128)).astype(BF)
    ok_first = splat(g != 0, (64, 128)).astype(BF)
    ok_last = splat(g != n_g - 1, (64, 128)).astype(BF)

    def field(p, t):
        tile = field_t[p, t]
        if t == 0:
            tile = tile * ok_low
        if t == 5:
            tile = tile * ok_high
        if p < 2:
            tile = tile * ok_first
        if p >= 6:
            tile = tile * ok_last
        return tile

    turn = [0]

    def conv_part(load, weight, runs):
        x_ref = x_v.at[turn[0] % 2]
        turn[0] += 1
        start = 0
        for p, first, last in runs:
            stack_rows([load(p, t) for t in range(first, last + 2)], x_ref, start)
            start += (last + 1 - first) * 128
        total = dot(weight[...], x_ref[:, 0:start])
        start = 0
        for p, first, last in runs:
            size = (last + 1 - first) * 128
            y_v[p, :, first * 128 : first * 128 + size] = total[:, start : start + size]
            start += size

    loads[1].wait()
    pack_taps(raw_first, k_first)
    conv_part(field, k_first, [(2, 1, 3), (3, 1, 3)])
    for d in order[:6]:
        sends[d].wait_send()
    for d in (2, 1, 3):
        peer = near(0, d)
        fine_sends.append(
            pltpu.make_async_remote_copy(
                src_ref=fine.at[0, pl.ds(2 * peer[1], 2)],
                dst_ref=fine_i.at[h],
                send_sem=f_send.at[d - 1],
                recv_sem=f_recv.at[d - 1],
                device_id=peer,
                device_id_type=MESH,
            )
        )
        fine_sends[-1].start()

    conv_part(field, k_first, [(4, 1, 3), (5, 1, 3)])

    for copy in loads[2:]:
        copy.wait()
    pack_taps(raw_coarse, k_coarse)
    pack_taps(raw_second, k_second)
    pack_taps(raw_refine, k_refine)
    k_restrict[...] = jnp.concatenate([raw_restrict[t] for t in range(8)], axis=1)
    for p in range(2):
        k_prolong[p * 64 : p * 64 + 64, :] = jnp.concatenate(
            [raw_prolong[p * 4 + t] for t in range(4)], axis=1
        )

    for copy in list_sends:
        copy.wait_recv()
    entry = lax.broadcasted_iota(jnp.int32, (8, 128), 1)
    lane = lanes_of((1, 128)).astype(F32)
    line = jnp.floor((lane + 0.5) * (1.0 / 6.0))
    place_x = lane - 6.0 * line - 1.0
    source = lax.broadcasted_iota(jnp.int32, (640, 128), 0).astype(F32)
    target = lanes_of((64, 512)).astype(F32)
    inner = (lax.broadcasted_iota(jnp.int32, (64, 1), 0) % 16).astype(F32)
    inner_y = jnp.floor(inner * 0.25)
    inner = inner_y * 64.0 + (inner - 4.0 * inner_y)
    for k in range(4):
        ids = lists[k].astype(F32)
        for s in range(2):
            at = k * 2 + s
            value = jnp.sum(
                jnp.where(entry == h * 2 + s, ids, 0.0), axis=1, keepdims=True
            )[0:1]
            py = jnp.floor(value * (1.0 / 16.0))
            px4 = 4.0 * (value - 16.0 * py)
            top = 256.0 * (py - 2.0 * h.astype(F32))
            col = place_x + px4
            want = jnp.where(
                (lane < 36.0) & (col >= 0.0) & (col < 64.0), line * 64.0 + col + top, -1.0
            )
            pick[:, at * 128 : at * 128 + 128] = jnp.where(source == want, 1.0, 0.0).astype(BF)
            want = jnp.where(value >= 0.0, inner + px4 + top, -1.0)
            place[at * 64 : at * 64 + 64, :] = jnp.where(target == want, 1.0, 0.0).astype(BF)
            live_v[k, s : s + 1, :] = jnp.where(
                jnp.broadcast_to(value, (1, 128)) >= 0.0, 1.0, 0.0
            )

    for d in ((0, -1), (0, 1)):
        sends[d].wait_recv()
    conv_part(field, k_first, [(p, t, t) for p in (2, 3, 4, 5) for t in (0, 4)])
    for d in order[:4] + order[6:]:
        sends[d].wait_recv()
    conv_part(field, k_first, [(0, 0, 4), (1, 0, 4)])
    conv_part(field, k_first, [(6, 0, 4), (7, 0, 4)])

    ok_rows = [jnp.ones((64, 128), F32)] * 5
    half = lanes_of((64, 128))
    ok_rows[0] = jnp.where((half < 64) & (h == 0), 0.0, 1.0)
    ok_rows[4] = jnp.where((half >= 64) & (h == n_h - 1), 0.0, 1.0)
    for q in range(6):
        for t in range(5):
            at = slice(t * 128, t * 128 + 128)
            value = silu(y_v[q, 0:64, at] + y_v[q + 1, 64:128, at] + y_v[q + 2, 128:192, at])
            if t in (0, 4):
                value = value * ok_rows[t]
            if q in (0, 5):
                value = value * splat(g != (0 if q == 0 else n_g - 1), (64, 128))
            act[q * 64 : q * 64 + 64, at] = value.astype(BF)

    parted = dot(act[64:320, :], split_v[...]).astype(BF)
    gathered = jnp.concatenate(
        [
            jnp.concatenate(
                [
                    parted[(2 * i + p) * 64 : (2 * i + p) * 64 + 64, f * 128 : f * 128 + 128]
                    for p in range(2)
                    for f in range(4)
                ],
                axis=0,
            )
            for i in range(2)
        ],
        axis=1,
    )
    reduced = dot(k_restrict[...], gathered).astype(BF)
    low = half < 64
    one, two = reduced[:, 0:128], reduced[:, 128:256]
    coarse_i[2] = one
    coarse_i[3] = two
    edge_o[0] = jnp.where(low, one, pltpu.roll(two, 64, 1))
    edge_o[1] = jnp.where(low, pltpu.roll(one, 64, 1), two)
    in_sends = []
    for i, (dz, dy) in enumerate(DIRS):
        if dy == 0:
            src, dst = coarse_i.at[pl.ds(2, 2)], coarse_i.at[pl.ds(2 - 2 * dz, 2)]
        else:
            src, dst = edge_o.at[(1 + dy) // 2], edge_i.at[(1 - dy) // 2, 1 - dz]
        in_sends.append(
            pltpu.make_async_remote_copy(
                src_ref=src,
                dst_ref=dst,
                send_sem=c_send.at[i],
                recv_sem=c_recv.at[i],
                device_id=near(dz, dy),
                device_id_type=MESH,
            )
        )
    for i in (0, 2, 5, 7, 3, 4, 1, 6):
        in_sends[i].start()

    for k in range(4):
        found = dot(act[...], pick[:, k * 256 : k * 256 + 256])
        for s in range(2):
            parts = [found[q * 64 : q * 64 + 64, s * 128 : s * 128 + 128] for q in range(6)]
            for t in range(2):
                tile = (
                    parts[3 * t]
                    + pltpu.roll(parts[3 * t + 1], 40, 1)
                    + pltpu.roll(parts[3 * t + 2], 80, 1)
                )
                at = (k * 2 + s) * 64
                win[t, at : at + 64, :] = tile.astype(BF)

    own_fine.wait()
    for copy in fine_sends:
        copy.wait_recv()
    for m in range(5):
        if m < 4:
            left = fine_i[:, :, :, m * 128 : m * 128 + 128].reshape(512, 128)
            right = win[(m + 1) // 3]
        else:
            left = win[0]
            right = win[1]
        spread = dot(jnp.concatenate([left, right], axis=1), block_v[m]).astype(BF)
        for s in range(8):
            for tap in range(9):
                xf_v[s, tap * 64 : tap * 64 + 64, m * 128 : m * 128 + 128] = spread[
                    s * 64 : s * 64 + 64, tap * 128 : tap * 128 + 128
                ]

    low = lanes_of((64, 128)) < 64
    back_sends = []
    for d in (2, 1, 3, 0):
        peer = near(0, d)
        k = peer[1]
        for s in range(2):
            total = dot(k_refine[...], xf_v[k * 2 + s])
            alive = jnp.broadcast_to(live_v[k, s : s + 1, :], (64, 128)) > 0.5
            behind = [total[0:64, m * 128 : m * 128 + 128] for m in range(5)]
            ahead = [total[128:192, m * 128 : m * 128 + 128] for m in range(5)]
            behind_r = [pltpu.roll(v, 64, 1) for v in behind[:4]]
            ahead_r = [pltpu.roll(v, 64, 1) for v in ahead[:4]]
            for m in range(4):
                at = slice(m * 128, m * 128 + 128)
                value = total[64:128, at]
                value += jnp.where(low, behind_r[m - 1] if m > 0 else behind[4], behind_r[m])
                value += jnp.where(low, ahead_r[m], ahead_r[m + 1] if m < 3 else ahead[4])
                value += fine_i[k, s, :, at].astype(F32)
                value = jnp.where(alive, value, 0.0)
                fine_o[k, s, :, at] = value.astype(BF)
        if d == 0:
            continue
        back_sends.append(
            pltpu.make_async_remote_copy(
                src_ref=fine_o.at[k],
                dst_ref=fine_out.at[0, pl.ds(2 * h, 2)],
                send_sem=b_send.at[d - 1],
                recv_sem=b_recv.at[d - 1],
                device_id=peer,
                device_id_type=MESH,
            )
        )
        back_sends[-1].start()
    own_store = pltpu.make_async_copy(
        fine_o.at[h], fine_out.at[0, pl.ds(2 * h, 2)], store_sem.at[0]
    )
    own_store.start()
    means = dot(fine_o[...].reshape(512, 512), mean_v[...])
    back = jnp.concatenate(
        [
            (
                means[k * 128 : k * 128 + 64]
                + pltpu.roll(means[k * 128 + 64 : k * 128 + 128], 64, 1)
            ).astype(BF)
            for k in range(4)
        ],
        axis=1,
    )
    wide = lanes_of((64, 512)) % 64 // 16
    zero = jnp.zeros_like(back)
    ones = jnp.where(lanes_of((16, 512)) % 64 < 16, 1.0, 0.0).astype(BF)
    stacked = jnp.concatenate([jnp.where(wide == z, back, zero) for z in range(4)] + [ones], axis=0)
    placed = dot(stacked, place[...])

    for copy in in_sends:
        copy.wait_recv()
    x_ref = x_v.at[turn[0] % 2]
    turn[0] += 1
    for i in range(6):
        before, mid, after = edge_i[0, i // 2], coarse_i[i], edge_i[1, i // 2]
        if i < 2:
            before, mid, after = before * ok_first, mid * ok_first, after * ok_first
        if i >= 4:
            before, mid, after = before * ok_last, mid * ok_last, after * ok_last
        before, after = before * ok_low, after * ok_high
        mid_r = pltpu.roll(mid, 64, 1)
        around = [
            jnp.where(low, pltpu.roll(before, 64, 1) if i % 2 else before, mid_r),
            jnp.where(
                half < 32, pltpu.roll(before, 32 if i % 2 else 96, 1), pltpu.roll(mid, 32, 1)
            ),
            mid,
            jnp.where(half < 96, pltpu.roll(mid, 96, 1), pltpu.roll(after, 32 if i % 2 else 96, 1)),
            jnp.where(low, mid_r, after if i % 2 else pltpu.roll(after, 64, 1)),
        ]
        for a, tile in enumerate(around):
            for dx, moved in enumerate(shifted(tile, 32)):
                for part, dy in ((0, a), (1, a - 2)):
                    if 0 <= dy < 3:
                        at = slice(i * 256 + part * 128, i * 256 + part * 128 + 128)
                        tap = dy * 3 + dx
                        x_ref[tap * 64 : tap * 64 + 64, at] = moved
    total = dot(k_coarse[...], x_ref[...])
    no_row = jnp.where((half < 32) & (h == 0), 0.0, 1.0)
    no_end = jnp.where((half >= 96) & (h == n_h - 1), 0.0, 1.0)
    rows = []
    for i in range(4):
        parts = []
        for part in range(2):
            at = i * 256 + part * 128
            value = silu(
                total[0:64, at : at + 128]
                + total[64:128, at + 256 : at + 384]
                + total[128:192, at + 512 : at + 640]
            )
            value = value * (no_row if part == 0 else no_end)
            if i in (0, 3):
                value = value * splat(g != (0 if i == 0 else n_g - 1), (64, 128))
            parts.append(value.astype(BF))
        rows += [parts[0]] + [pltpu.roll(parts[0], 128 - 32 * j, 1) for j in range(1, 4)]
        rows += [pltpu.roll(parts[1], 128 - 32 * j, 1) for j in range(2, 4)]
    spread = dot(jnp.concatenate(rows, axis=0), spread_v[...]).astype(BF)
    for i in range(4):
        for t in range(5):
            for f in range(4):
                row = (i * 6 + t + 1 - f // 2) * 64
                at = i * 640 + t * 128
                u_v[f * 64 : f * 64 + 64, at : at + 128] = spread[
                    row : row + 64, f * 128 : f * 128 + 128
                ]
    for i in range(4):
        lifted = dot(k_prolong[...], u_v[:, i * 640 : i * 640 + 640])
        for p in range(2):
            q = 2 * i - 1 + p
            if 0 <= q <= 5:
                at = slice(q * 64, q * 64 + 64)
                summed[at, :] = (
                    act[at, :].astype(F32) + lifted[p * 64 : p * 64 + 64, :]
                ).astype(BF)

    def total_in(q, t):
        return summed[q * 64 : q * 64 + 64, t * 128 : t * 128 + 128]

    for q in (0, 2, 4):
        conv_part(total_in, k_second, [(q, 0, 3), (q + 1, 0, 3)])

    for z in range(4):
        for j in range(4):
            at = slice(j * 128, j * 128 + 128)
            value = y_v[z, 0:64, at] + y_v[z + 1, 64:128, at] + y_v[z + 2, 128:192, at]
            value += field_t[2 + z, 1 + j].astype(F32)
            covered = jnp.broadcast_to(placed[256:257, at], (64, 128)) > 0.5
            value = jnp.where(covered, placed[z * 64 : z * 64 + 64, at], value)
            cells[pl.ds(z * 8 + 2 * j, 64, stride=32), :] = value[:, 0:64]
            cells[pl.ds(z * 8 + 2 * j + 1, 64, stride=32), :] = value[:, 64:128]
    fields_v[...] = cells[...].reshape(64, 4, 8, 64).astype(BF)
    base_store = pltpu.make_async_copy(fields_v, base_out, store_sem.at[1])
    base_store.start()
    for copy in back_sends:
        copy.wait_recv()
    for d in order[6:]:
        sends[d].wait_send()
    for copy in list_sends + fine_sends + in_sends + back_sends:
        copy.wait_send()
    own_store.wait()
    base_store.wait()


def finish(base, fine, base_out, fine_out, base_v, fine_v, in_sems, out_sems):
    loads = []
    stores = []
    for i in range(4):
        parts = [
            (base, base_v, base_out, (pl.ds(16 * i, 16),)),
            (fine, fine_v, fine_out, (pl.ds(0, 1), pl.ds(2 * i, 2))),
        ]
        for j, (src, mid, dst, at) in enumerate(parts):
            loads.append(pltpu.make_async_copy(src.at[at], mid.at[at], in_sems.at[2 * i + j]))
            stores.append(pltpu.make_async_copy(mid.at[at], dst.at[at], out_sems.at[2 * i + j]))
    for copy in loads:
        copy.start()
    for load, store in zip(loads, stores):
        load.wait()
        store.start()
    for copy in stores:
        copy.wait()


def body(
    fields,
    block_patch,
    fine_in,
    conv_first,
    restrict_weight,
    coarse_weight,
    prolong_weight,
    conv_second,
    refine_weight,
):
    any_spec = pl.BlockSpec(memory_space=pl.ANY)
    vmem_spec = pl.BlockSpec(memory_space=pltpu.VMEM)
    dma = pltpu.SemaphoreType.DMA
    v = pltpu.VMEM
    results = pl.pallas_call(
        kernel,
        out_shape=[
            jax.ShapeDtypeStruct(fields.shape, BF),
            jax.ShapeDtypeStruct(fine_in.shape, BF),
        ],
        in_specs=[any_spec, vmem_spec] + [any_spec] * 11,
        out_specs=[any_spec, any_spec],
        scratch_shapes=[
            v((64, 4, 8, 64), BF),
            v((2048, 64), F32),
            v((8, 6, 64, 128), BF),
            v((27, 64, 64), BF),
            v((8, 64, 64), BF),
            v((27, 64, 64), BF),
            v((8, 64, 64), BF),
            v((27, 64, 64), BF),
            v((27, 64, 64), BF),
            v((640, 512), BF),
            v((128, 512), BF),
            v((512, 128), BF),
            v((5, 256, 1152), BF),
            v((4, 2, 64, 512), BF),
            v((4, 2, 64, 512), BF),
            v((192, 576), BF),
            v((64, 512), BF),
            v((192, 576), BF),
            v((128, 256), BF),
            v((192, 576), BF),
            v((192, 576), BF),
            v((4, 8, 128), jnp.int32),
            v((4, 8, 128), F32),
            v((640, 1024), BF),
            v((512, 512), BF),
            v((2, 576, 1536), BF),
            v((8, 192, 640), F32),
            v((384, 640), BF),
            v((384, 640), BF),
            v((6, 64, 128), BF),
            v((2, 64, 128), BF),
            v((2, 3, 64, 128), BF),
            v((256, 2560), BF),
            v((2, 512, 128), BF),
            v((8, 576, 640), BF),
            dma((11,)),
            dma((1,)),
            dma((2,)),
            dma((8,)),
            dma((8,)),
            dma((8,)),
            dma((8,)),
            dma((3,)),
            dma((3,)),
            dma((3,)),
            dma((3,)),
            dma((3,)),
            dma((3,)),
        ],
        compiler_params=pltpu.CompilerParams(
            collective_id=0, has_side_effects=True, vmem_limit_bytes=64 * 1024 * 1024
        ),
        cost_estimate=pl.CostEstimate(flops=8 * 10**9, bytes_accessed=8 * 10**6, transcendentals=0),
    )(
        fields,
        block_patch,
        fine_in,
        conv_first,
        restrict_weight,
        coarse_weight,
        prolong_weight,
        conv_second,
        refine_weight,
        jnp.asarray(split_table(), BF),
        jnp.asarray(spread_table(), BF),
        jnp.asarray(mean_table(), BF),
        jnp.asarray(block_table(), BF),
    )
    return pl.pallas_call(
        finish,
        out_shape=[
            jax.ShapeDtypeStruct(fields.shape, BF),
            jax.ShapeDtypeStruct(fine_in.shape, BF),
        ],
        in_specs=[any_spec, any_spec],
        out_specs=[any_spec, any_spec],
        scratch_shapes=[
            v(fields.shape, BF),
            v(fine_in.shape, BF),
            dma((8,)),
            dma((8,)),
        ],
        compiler_params=pltpu.CompilerParams(vmem_limit_bytes=64 * 1024 * 1024),
    )(*results)


def solution(mesh):
    in_specs = (
        P(None, "gz", "gx", None),
        P("gz", "gx"),
        P("gz", "gx", None, None),
        P(),
        P(),
        P(),
        P(),
        P(),
        P(),
    )
    out_specs = (P(None, "gz", "gx", None), P("gz", "gx", None, None))
    return jax.shard_map(body, mesh=mesh, in_specs=in_specs, out_specs=out_specs, check_vma=False)
```

```python
import jax
import jax.numpy as jnp
import numpy as np
from jax import lax
from jax.experimental import pallas as pl
from jax.experimental.pallas import tpu as pltpu
from jax.sharding import PartitionSpec as P

BF = jnp.bfloat16
F32 = jnp.float32
MESH = pl.DeviceIdType.MESH
DIRS = [(dz, dy) for dz in (-1, 0, 1) for dy in (-1, 0, 1) if (dz, dy) != (0, 0)]


def split_table():
    cell = np.arange(512)
    row, col = cell // 64, cell % 64
    table = np.zeros((640, 512), np.float32)
    table[cell + 64, ((row % 2) * 2 + col % 2) * 128 + (row // 2) * 32 + col // 2] = 1
    return table


def spread_table():
    table = np.zeros((128, 512), np.float32)
    for q in range(2):
        for r in range(2):
            for k in range(32):
                table[k, (q * 2 + r) * 128 + (1 - q) * 64 + 2 * k + r] = 1
    return table


def mean_table():
    cell = np.arange(512)
    z, y, x = cell // 64, cell // 8 % 8, cell % 8
    table = np.zeros((512, 128), np.float32)
    table[cell, (z // 2) * 16 + (y // 2) * 4 + x // 2] = 0.125
    return table


def block_table():
    table = np.zeros((5, 256, 1152), np.float32)
    for m in range(5):
        for tap in range(9):
            for a in range(2):
                for b in range(8):
                    for e in range(8):
                        y, x = b + tap // 3 - 1, e + tap % 3 - 1
                        col = tap * 128 + a * 64 + b * 8 + e
                        ghost = (y // 2 + 1) * 6 + x // 2 + 1
                        if m == 4:
                            table[m, a * 128 + (0, 80)[a] + ghost, col] = 1
                        elif 0 <= y < 8 and 0 <= x < 8:
                            table[m, a * 64 + y * 8 + x, col] = 1
                        else:
                            table[m, 128 + 40 * ((m + 1) % 3) + ghost, col] = 1
    return table


def dot(a, b):
    return jnp.dot(a, b, preferred_element_type=F32)


def silu(v):
    return v / (1.0 + jnp.exp(-v))


def lanes_of(shape):
    return lax.broadcasted_iota(jnp.int32, shape, len(shape) - 1)


def splat(flag, shape):
    return jnp.full(shape, jnp.where(flag, 1.0, 0.0).astype(F32), F32)


def pack_taps(raw, packed):
    for dz in range(3):
        packed[dz * 64 : dz * 64 + 64, :] = jnp.concatenate(
            [raw[dz * 9 + t] for t in range(9)], axis=1
        )


def shifted(tile, period):
    lane = lanes_of(tile.shape) % period
    zero = jnp.zeros_like(tile)
    left = jnp.where(lane != 0, pltpu.roll(tile, 1, 1), zero)
    right = jnp.where(lane != period - 1, pltpu.roll(tile, 127, 1), zero)
    return left, tile, right


def stack_rows(tiles, x_ref, start):
    low = lanes_of((64, 128)) < 64
    moved = [shifted(t, 64) for t in tiles]
    for dx in range(3):
        swapped = [pltpu.roll(m[dx], 64, 1) for m in moved]
        for t in range(len(tiles) - 1):
            at = slice(start + t * 128, start + t * 128 + 128)
            x_ref[dx * 64 : dx * 64 + 64, at] = moved[t][dx]
            x_ref[192 + dx * 64 : 256 + dx * 64, at] = jnp.where(low, swapped[t], swapped[t + 1])
            x_ref[384 + dx * 64 : 448 + dx * 64, at] = moved[t + 1][dx]


def kernel(
    fields,
    patch,
    fine,
    w_first,
    w_restrict,
    w_coarse,
    w_prolong,
    w_second,
    w_refine,
    t_split,
    t_spread,
    t_mean,
    t_block,
    base_out,
    fine_out,
    fields_v,
    cells,
    field_t,
    raw_first,
    raw_restrict,
    raw_coarse,
    raw_prolong,
    raw_second,
    raw_refine,
    split_v,
    spread_v,
    mean_v,
    block_v,
    fine_i,
    fine_o,
    k_first,
    k_restrict,
    k_coarse,
    k_prolong,
    k_second,
    k_refine,
    lists,
    live_v,
    pick,
    place,
    x_v,
    y_v,
    act,
    summed,
    coarse_i,
    edge_o,
    edge_i,
    u_v,
    win,
    xf_v,
    load_sem,
    own_sem,
    store_sem,
    s_send,
    s_recv,
    c_send,
    c_recv,
    l_send,
    l_recv,
    f_send,
    f_recv,
    b_send,
    b_recv,
):
    g = lax.axis_index("gz")
    h = lax.axis_index("gx")
    n_g = lax.axis_size("gz")
    n_h = lax.axis_size("gx")

    def near(dz, dy):
        return (lax.rem(g + dz + n_g, n_g), lax.rem(h + dy + n_h, n_h))

    barrier = pltpu.get_barrier_semaphore()
    partners = DIRS + [(0, 2)]
    for dz, dy in partners:
        pl.semaphore_signal(barrier, inc=1, device_id=near(dz, dy), device_id_type=MESH)

    loads = []
    for i, (src, dst) in enumerate(
        [
            (fields, fields_v),
            (w_first, raw_first),
            (w_restrict, raw_restrict),
            (t_split, split_v),
            (w_refine, raw_refine),
            (t_block, block_v),
            (w_coarse, raw_coarse),
            (w_prolong, raw_prolong),
            (w_second, raw_second),
            (t_spread, spread_v),
            (t_mean, mean_v),
        ]
    ):
        loads.append(pltpu.make_async_copy(src, dst, load_sem.at[i]))
    loads[0].start()
    own_fine = pltpu.make_async_copy(
        fine.at[0, pl.ds(2 * h, 2)], fine_i.at[h], own_sem.at[0]
    )

    lists[h] = jnp.zeros((8, 128), jnp.int32)
    lists[h, 0:1, 0:8] = patch[...]

    loads[0].wait()
    for copy in loads[1:] + [own_fine]:
        copy.start()
    cells[...] = fields_v[...].astype(F32).reshape(2048, 64)
    for z in range(4):
        for j in range(4):
            pair = [cells[pl.ds(z * 8 + 2 * j + q, 64, stride=32), :] for q in range(2)]
            field_t[2 + z, 1 + j] = jnp.concatenate(pair, axis=1).astype(BF)

    pl.semaphore_wait(barrier, len(partners))

    def span_of(d, own, width, low, high):
        if d == 0:
            return pl.ds(low, own), pl.ds(low, own)
        if d > 0:
            return pl.ds(low + own - width, width), pl.ds(low - width, width)
        return pl.ds(low, width), pl.ds(high, width)

    sends = {}
    for i, (dz, dy) in enumerate(DIRS):
        zs, zd = span_of(dz, 4, 2, 2, 6)
        ys, yd = span_of(dy, 4, 1, 1, 5)
        sends[dz, dy] = pltpu.make_async_remote_copy(
            src_ref=field_t.at[zs, ys],
            dst_ref=field_t.at[zd, yd],
            send_sem=s_send.at[i],
            recv_sem=s_recv.at[i],
            device_id=near(dz, dy),
            device_id_type=MESH,
        )
    order = [(-1, -1), (-1, 1), (1, -1), (1, 1), (0, -1), (0, 1), (-1, 0), (1, 0)]
    for d in order:
        sends[d].start()
    list_sends = []
    fine_sends = []
    for d in (2, 1, 3):
        peer = near(0, d)
        list_sends.append(
            pltpu.make_async_remote_copy(
                src_ref=lists.at[h],
                dst_ref=lists.at[h],
                send_sem=l_send.at[d - 1],
                recv_sem=l_recv.at[d - 1],
                device_id=peer,
                device_id_type=MESH,
            )
        )
        list_sends[-1].start()
    first_z, last_z = g == 0, g == n_g - 1
    ok_low = splat(h != 0, (64, 128)).astype(BF)
    ok_high = splat(h != n_h - 1, (64, 128)).astype(BF)
    ok_first = splat(g != 0, (64, 128)).astype(BF)
    ok_last = splat(g != n_g - 1, (64, 128)).astype(BF)

    def field(p, t):
        tile = field_t[p, t]
        if t == 0:
            tile = tile * ok_low
        if t == 5:
            tile = tile * ok_high
        if p < 2:
            tile = tile * ok_first
        if p >= 6:
            tile = tile * ok_last
        return tile

    turn = [0]

    def conv_part(load, weight, runs):
        x_ref = x_v.at[turn[0] % 2]
        turn[0] += 1
        start = 0
        for p, first, last in runs:
            stack_rows([load(p, t) for t in range(first, last + 2)], x_ref, start)
            start += (last + 1 - first) * 128
        total = dot(weight[...], x_ref[:, 0:start])
        start = 0
        for p, first, last in runs:
            size = (last + 1 - first) * 128
            y_v[p, :, first * 128 : first * 128 + size] = total[:, start : start + size]
            start += size

    loads[1].wait()
    pack_taps(raw_first, k_first)
    conv_part(field, k_first, [(2, 1, 3), (3, 1, 3)])
    for d in order[:6]:
        sends[d].wait_send()
    for d in (2, 1, 3):
        peer = near(0, d)
        fine_sends.append(
            pltpu.make_async_remote_copy(
                src_ref=fine.at[0, pl.ds(2 * peer[1], 2)],
                dst_ref=fine_i.at[h],
                send_sem=f_send.at[d - 1],
                recv_sem=f_recv.at[d - 1],
                device_id=peer,
                device_id_type=MESH,
            )
        )
        fine_sends[-1].start()

    conv_part(field, k_first, [(4, 1, 3), (5, 1, 3)])

    for copy in loads[2:]:
        copy.wait()
    pack_taps(raw_coarse, k_coarse)
    pack_taps(raw_second, k_second)
    pack_taps(raw_refine, k_refine)
    k_restrict[...] = jnp.concatenate([raw_restrict[t] for t in range(8)], axis=1)
    for p in range(2):
        k_prolong[p * 64 : p * 64 + 64, :] = jnp.concatenate(
            [raw_prolong[p * 4 + t] for t in range(4)], axis=1
        )

    for copy in list_sends:
        copy.wait_recv()
    entry = lax.broadcasted_iota(jnp.int32, (8, 128), 1)
    lane = lanes_of((1, 128)).astype(F32)
    line = jnp.floor((lane + 0.5) * (1.0 / 6.0))
    place_x = lane - 6.0 * line - 1.0
    source = lax.broadcasted_iota(jnp.int32, (640, 128), 0).astype(F32)
    target = lanes_of((64, 512)).astype(F32)
    inner = (lax.broadcasted_iota(jnp.int32, (64, 1), 0) % 16).astype(F32)
    inner_y = jnp.floor(inner * 0.25)
    inner = inner_y * 64.0 + (inner - 4.0 * inner_y)
    for k in range(4):
        ids = lists[k].astype(F32)
        for s in range(2):
            at = k * 2 + s
            value = jnp.sum(
                jnp.where(entry == h * 2 + s, ids, 0.0), axis=1, keepdims=True
            )[0:1]
            py = jnp.floor(value * (1.0 / 16.0))
            px4 = 4.0 * (value - 16.0 * py)
            top = 256.0 * (py - 2.0 * h.astype(F32))
            col = place_x + px4
            want = jnp.where(
                (lane < 36.0) & (col >= 0.0) & (col < 64.0), line * 64.0 + col + top, -1.0
            )
            pick[:, at * 128 : at * 128 + 128] = jnp.where(source == want, 1.0, 0.0).astype(BF)
            want = jnp.where(value >= 0.0, inner + px4 + top, -1.0)
            place[at * 64 : at * 64 + 64, :] = jnp.where(target == want, 1.0, 0.0).astype(BF)
            live_v[k, s : s + 1, :] = jnp.where(
                jnp.broadcast_to(value, (1, 128)) >= 0.0, 1.0, 0.0
            )

    for d in ((0, -1), (0, 1)):
        sends[d].wait_recv()
    conv_part(field, k_first, [(p, t, t) for p in (2, 3, 4, 5) for t in (0, 4)])
    for d in order[:4] + order[6:]:
        sends[d].wait_recv()
    conv_part(field, k_first, [(0, 0, 4), (1, 0, 4)])
    conv_part(field, k_first, [(6, 0, 4), (7, 0, 4)])

    ok_rows = [jnp.ones((64, 128), F32)] * 5
    half = lanes_of((64, 128))
    ok_rows[0] = jnp.where((half < 64) & (h == 0), 0.0, 1.0)
    ok_rows[4] = jnp.where((half >= 64) & (h == n_h - 1), 0.0, 1.0)
    for q in range(6):
        for t in range(5):
            at = slice(t * 128, t * 128 + 128)
            value = silu(y_v[q, 0:64, at] + y_v[q + 1, 64:128, at] + y_v[q + 2, 128:192, at])
            if t in (0, 4):
                value = value * ok_rows[t]
            if q in (0, 5):
                value = value * splat(g != (0 if q == 0 else n_g - 1), (64, 128))
            act[q * 64 : q * 64 + 64, at] = value.astype(BF)

    parted = dot(act[64:320, :], split_v[...]).astype(BF)
    gathered = jnp.concatenate(
        [
            jnp.concatenate(
                [
                    parted[(2 * i + p) * 64 : (2 * i + p) * 64 + 64, f * 128 : f * 128 + 128]
                    for p in range(2)
                    for f in range(4)
                ],
                axis=0,
            )
            for i in range(2)
        ],
        axis=1,
    )
    reduced = dot(k_restrict[...], gathered).astype(BF)
    low = half < 64
    one, two = reduced[:, 0:128], reduced[:, 128:256]
    coarse_i[2] = one
    coarse_i[3] = two
    edge_o[0] = jnp.where(low, one, pltpu.roll(two, 64, 1))
    edge_o[1] = jnp.where(low, pltpu.roll(one, 64, 1), two)
    in_sends = []
    for i, (dz, dy) in enumerate(DIRS):
        if dy == 0:
            src, dst = coarse_i.at[pl.ds(2, 2)], coarse_i.at[pl.ds(2 - 2 * dz, 2)]
        else:
            src, dst = edge_o.at[(1 + dy) // 2], edge_i.at[(1 - dy) // 2, 1 - dz]
        in_sends.append(
            pltpu.make_async_remote_copy(
                src_ref=src,
                dst_ref=dst,
                send_sem=c_send.at[i],
                recv_sem=c_recv.at[i],
                device_id=near(dz, dy),
                device_id_type=MESH,
            )
        )
    for i in (0, 2, 5, 7, 3, 4, 1, 6):
        in_sends[i].start()

    for k in range(4):
        found = dot(act[...], pick[:, k * 256 : k * 256 + 256])
        for s in range(2):
            parts = [found[q * 64 : q * 64 + 64, s * 128 : s * 128 + 128] for q in range(6)]
            for t in range(2):
                tile = (
                    parts[3 * t]
                    + pltpu.roll(parts[3 * t + 1], 40, 1)
                    + pltpu.roll(parts[3 * t + 2], 80, 1)
                )
                at = (k * 2 + s) * 64
                win[t, at : at + 64, :] = tile.astype(BF)

    own_fine.wait()
    for copy in fine_sends:
        copy.wait_recv()
    def spread_blocks(d_first, d_second):
        ks = [near(0, d)[1] for d in (d_first, d_second)]
        sides = [
            jnp.concatenate([win[t, pl.ds(pl.multiple_of(k * 128, 128), 128), :] for k in ks], axis=0)
            for t in range(2)
        ]
        for m in range(5):
            if m < 4:
                left = jnp.concatenate(
                    [
                        fine_i[k, :, :, m * 128 : m * 128 + 128].reshape(128, 128)
                        for k in ks
                    ],
                    axis=0,
                )
                right = sides[(m + 1) // 3]
            else:
                left, right = sides
            spread = dot(jnp.concatenate([left, right], axis=1), block_v[m]).astype(BF)
            for i, d in enumerate((d_first, d_second)):
                for s in range(2):
                    row = i * 128 + s * 64
                    for tap in range(9):
                        xf_v[d * 2 + s, tap * 64 : tap * 64 + 64, m * 128 : m * 128 + 128] = spread[
                            row : row + 64, tap * 128 : tap * 128 + 128
                        ]

    low = lanes_of((64, 128)) < 64
    back_sends = []
    for d in (2, 1, 3, 0):
        if d in (2, 3):
            spread_blocks(d, 1 if d == 2 else 0)
        peer = near(0, d)
        k = peer[1]
        for s in range(2):
            total = dot(k_refine[...], xf_v[d * 2 + s])
            alive = jnp.broadcast_to(live_v[k, s : s + 1, :], (64, 128)) > 0.5
            behind = [total[0:64, m * 128 : m * 128 + 128] for m in range(5)]
            ahead = [total[128:192, m * 128 : m * 128 + 128] for m in range(5)]
            behind_r = [pltpu.roll(v, 64, 1) for v in behind[:4]]
            ahead_r = [pltpu.roll(v, 64, 1) for v in ahead[:4]]
            for m in range(4):
                at = slice(m * 128, m * 128 + 128)
                value = total[64:128, at]
                value += jnp.where(low, behind_r[m - 1] if m > 0 else behind[4], behind_r[m])
                value += jnp.where(low, ahead_r[m], ahead_r[m + 1] if m < 3 else ahead[4])
                value += fine_i[k, s, :, at].astype(F32)
                value = jnp.where(alive, value, 0.0)
                fine_o[k, s, :, at] = value.astype(BF)
        if d == 0:
            continue
        back_sends.append(
            pltpu.make_async_remote_copy(
                src_ref=fine_o.at[k],
                dst_ref=fine_out.at[0, pl.ds(2 * h, 2)],
                send_sem=b_send.at[d - 1],
                recv_sem=b_recv.at[d - 1],
                device_id=peer,
                device_id_type=MESH,
            )
        )
        back_sends[-1].start()
    own_store = pltpu.make_async_copy(
        fine_o.at[h], fine_out.at[0, pl.ds(2 * h, 2)], store_sem.at[0]
    )
    own_store.start()
    means = dot(fine_o[...].reshape(512, 512), mean_v[...])
    back = jnp.concatenate(
        [
            (
                means[k * 128 : k * 128 + 64]
                + pltpu.roll(means[k * 128 + 64 : k * 128 + 128], 64, 1)
            ).astype(BF)
            for k in range(4)
        ],
        axis=1,
    )
    wide = lanes_of((64, 512)) % 64 // 16
    zero = jnp.zeros_like(back)
    ones = jnp.where(lanes_of((16, 512)) % 64 < 16, 1.0, 0.0).astype(BF)
    stacked = jnp.concatenate([jnp.where(wide == z, back, zero) for z in range(4)] + [ones], axis=0)
    placed = dot(stacked, place[...])

    for copy in in_sends:
        copy.wait_recv()
    x_ref = x_v.at[turn[0] % 2]
    turn[0] += 1
    for i in range(6):
        before, mid, after = edge_i[0, i // 2], coarse_i[i], edge_i[1, i // 2]
        if i < 2:
            before, mid, after = before * ok_first, mid * ok_first, after * ok_first
        if i >= 4:
            before, mid, after = before * ok_last, mid * ok_last, after * ok_last
        before, after = before * ok_low, after * ok_high
        mid_r = pltpu.roll(mid, 64, 1)
        around = [
            jnp.where(low, pltpu.roll(before, 64, 1) if i % 2 else before, mid_r),
            jnp.where(
                half < 32, pltpu.roll(before, 32 if i % 2 else 96, 1), pltpu.roll(mid, 32, 1)
            ),
            mid,
            jnp.where(half < 96, pltpu.roll(mid, 96, 1), pltpu.roll(after, 32 if i % 2 else 96, 1)),
            jnp.where(low, mid_r, after if i % 2 else pltpu.roll(after, 64, 1)),
        ]
        for a, tile in enumerate(around):
            for dx, moved in enumerate(shifted(tile, 32)):
                for part, dy in ((0, a), (1, a - 2)):
                    if 0 <= dy < 3:
                        at = slice(i * 256 + part * 128, i * 256 + part * 128 + 128)
                        tap = dy * 3 + dx
                        x_ref[tap * 64 : tap * 64 + 64, at] = moved
    total = dot(k_coarse[...], x_ref[...])
    no_row = jnp.where((half < 32) & (h == 0), 0.0, 1.0)
    no_end = jnp.where((half >= 96) & (h == n_h - 1), 0.0, 1.0)
    rows = []
    for i in range(4):
        parts = []
        for part in range(2):
            at = i * 256 + part * 128
            value = silu(
                total[0:64, at : at + 128]
                + total[64:128, at + 256 : at + 384]
                + total[128:192, at + 512 : at + 640]
            )
            value = value * (no_row if part == 0 else no_end)
            if i in (0, 3):
                value = value * splat(g != (0 if i == 0 else n_g - 1), (64, 128))
            parts.append(value.astype(BF))
        rows += [parts[0]] + [pltpu.roll(parts[0], 128 - 32 * j, 1) for j in range(1, 4)]
        rows += [pltpu.roll(parts[1], 128 - 32 * j, 1) for j in range(2, 4)]
    spread = dot(jnp.concatenate(rows, axis=0), spread_v[...]).astype(BF)
    for i in range(4):
        for t in range(5):
            for f in range(4):
                row = (i * 6 + t + 1 - f // 2) * 64
                at = i * 640 + t * 128
                u_v[f * 64 : f * 64 + 64, at : at + 128] = spread[
                    row : row + 64, f * 128 : f * 128 + 128
                ]
    for i in range(4):
        lifted = dot(k_prolong[...], u_v[:, i * 640 : i * 640 + 640])
        for p in range(2):
            q = 2 * i - 1 + p
            if 0 <= q <= 5:
                at = slice(q * 64, q * 64 + 64)
                summed[at, :] = (
                    act[at, :].astype(F32) + lifted[p * 64 : p * 64 + 64, :]
                ).astype(BF)

    def total_in(q, t):
        return summed[q * 64 : q * 64 + 64, t * 128 : t * 128 + 128]

    for q in (0, 2, 4):
        conv_part(total_in, k_second, [(q, 0, 3), (q + 1, 0, 3)])

    for z in range(4):
        for j in range(4):
            at = slice(j * 128, j * 128 + 128)
            value = y_v[z, 0:64, at] + y_v[z + 1, 64:128, at] + y_v[z + 2, 128:192, at]
            value += field_t[2 + z, 1 + j].astype(F32)
            covered = jnp.broadcast_to(placed[256:257, at], (64, 128)) > 0.5
            value = jnp.where(covered, placed[z * 64 : z * 64 + 64, at], value)
            cells[pl.ds(z * 8 + 2 * j, 64, stride=32), :] = value[:, 0:64]
            cells[pl.ds(z * 8 + 2 * j + 1, 64, stride=32), :] = value[:, 64:128]
    fields_v[...] = cells[...].reshape(64, 4, 8, 64).astype(BF)
    base_store = pltpu.make_async_copy(fields_v, base_out, store_sem.at[1])
    base_store.start()
    for copy in back_sends:
        copy.wait_recv()
    for d in order[6:]:
        sends[d].wait_send()
    for copy in list_sends + fine_sends + in_sends + back_sends:
        copy.wait_send()
    own_store.wait()
    base_store.wait()


def finish(base, fine, base_out, fine_out, base_v, fine_v, in_sems, out_sems):
    loads = []
    stores = []
    for i in range(4):
        parts = [
            (base, base_v, base_out, (pl.ds(16 * i, 16),)),
            (fine, fine_v, fine_out, (pl.ds(0, 1), pl.ds(2 * i, 2))),
        ]
        for j, (src, mid, dst, at) in enumerate(parts):
            loads.append(pltpu.make_async_copy(src.at[at], mid.at[at], in_sems.at[2 * i + j]))
            stores.append(pltpu.make_async_copy(mid.at[at], dst.at[at], out_sems.at[2 * i + j]))
    for copy in loads:
        copy.start()
    for load, store in zip(loads, stores):
        load.wait()
        store.start()
    for copy in stores:
        copy.wait()


def body(
    fields,
    block_patch,
    fine_in,
    conv_first,
    restrict_weight,
    coarse_weight,
    prolong_weight,
    conv_second,
    refine_weight,
):
    any_spec = pl.BlockSpec(memory_space=pl.ANY)
    vmem_spec = pl.BlockSpec(memory_space=pltpu.VMEM)
    dma = pltpu.SemaphoreType.DMA
    v = pltpu.VMEM
    results = pl.pallas_call(
        kernel,
        out_shape=[
            jax.ShapeDtypeStruct(fields.shape, BF),
            jax.ShapeDtypeStruct(fine_in.shape, BF),
        ],
        in_specs=[any_spec, vmem_spec] + [any_spec] * 11,
        out_specs=[any_spec, any_spec],
        scratch_shapes=[
            v((64, 4, 8, 64), BF),
            v((2048, 64), F32),
            v((8, 6, 64, 128), BF),
            v((27, 64, 64), BF),
            v((8, 64, 64), BF),
            v((27, 64, 64), BF),
            v((8, 64, 64), BF),
            v((27, 64, 64), BF),
            v((27, 64, 64), BF),
            v((640, 512), BF),
            v((128, 512), BF),
            v((512, 128), BF),
            v((5, 256, 1152), BF),
            v((4, 2, 64, 512), BF),
            v((4, 2, 64, 512), BF),
            v((192, 576), BF),
            v((64, 512), BF),
            v((192, 576), BF),
            v((128, 256), BF),
            v((192, 576), BF),
            v((192, 576), BF),
            v((4, 8, 128), jnp.int32),
            v((4, 8, 128), F32),
            v((640, 1024), BF),
            v((512, 512), BF),
            v((2, 576, 1536), BF),
            v((8, 192, 640), F32),
            v((384, 640), BF),
            v((384, 640), BF),
            v((6, 64, 128), BF),
            v((2, 64, 128), BF),
            v((2, 3, 64, 128), BF),
            v((256, 2560), BF),
            v((2, 512, 128), BF),
            v((8, 576, 640), BF),
            dma((11,)),
            dma((1,)),
            dma((2,)),
            dma((8,)),
            dma((8,)),
            dma((8,)),
            dma((8,)),
            dma((3,)),
            dma((3,)),
            dma((3,)),
            dma((3,)),
            dma((3,)),
            dma((3,)),
        ],
        compiler_params=pltpu.CompilerParams(
            collective_id=0, has_side_effects=True, vmem_limit_bytes=64 * 1024 * 1024
        ),
        cost_estimate=pl.CostEstimate(flops=8 * 10**9, bytes_accessed=8 * 10**6, transcendentals=0),
    )(
        fields,
        block_patch,
        fine_in,
        conv_first,
        restrict_weight,
        coarse_weight,
        prolong_weight,
        conv_second,
        refine_weight,
        jnp.asarray(split_table(), BF),
        jnp.asarray(spread_table(), BF),
        jnp.asarray(mean_table(), BF),
        jnp.asarray(block_table(), BF),
    )
    return pl.pallas_call(
        finish,
        out_shape=[
            jax.ShapeDtypeStruct(fields.shape, BF),
            jax.ShapeDtypeStruct(fine_in.shape, BF),
        ],
        in_specs=[any_spec, any_spec],
        out_specs=[any_spec, any_spec],
        scratch_shapes=[
            v(fields.shape, BF),
            v(fine_in.shape, BF),
            dma((8,)),
            dma((8,)),
        ],
        compiler_params=pltpu.CompilerParams(vmem_limit_bytes=64 * 1024 * 1024),
    )(*results)


def solution(mesh):
    in_specs = (
        P(None, "gz", "gx", None),
        P("gz", "gx"),
        P("gz", "gx", None, None),
        P(),
        P(),
        P(),
        P(),
        P(),
        P(),
    )
    out_specs = (P(None, "gz", "gx", None), P("gz", "gx", None, None))
    return jax.shard_map(body, mesh=mesh, in_specs=in_specs, out_specs=out_specs, check_vma=False)
```

```python
import jax
import jax.numpy as jnp
import numpy as np
from jax import lax
from jax.experimental import pallas as pl
from jax.experimental.pallas import tpu as pltpu
from jax.sharding import PartitionSpec as P

BF = jnp.bfloat16
F32 = jnp.float32
MESH = pl.DeviceIdType.MESH
DIRS = [(dz, dy) for dz in (-1, 0, 1) for dy in (-1, 0, 1) if (dz, dy) != (0, 0)]


def split_table():
    cell = np.arange(512)
    row, col = cell // 64, cell % 64
    table = np.zeros((640, 512), np.float32)
    table[cell + 64, ((row % 2) * 2 + col % 2) * 128 + (row // 2) * 32 + col // 2] = 1
    return table


def spread_table():
    table = np.zeros((128, 512), np.float32)
    for q in range(2):
        for r in range(2):
            for k in range(32):
                table[k, (q * 2 + r) * 128 + (1 - q) * 64 + 2 * k + r] = 1
    return table


def mean_table():
    cell = np.arange(512)
    z, y, x = cell // 64, cell // 8 % 8, cell % 8
    table = np.zeros((512, 128), np.float32)
    table[cell, (z // 2) * 16 + (y // 2) * 4 + x // 2] = 0.125
    return table


def block_table():
    table = np.zeros((5, 256, 1152), np.float32)
    for m in range(5):
        for tap in range(9):
            for a in range(2):
                for b in range(8):
                    for e in range(8):
                        y, x = b + tap // 3 - 1, e + tap % 3 - 1
                        col = tap * 128 + a * 64 + b * 8 + e
                        ghost = (y // 2 + 1) * 6 + x // 2 + 1
                        if m == 4:
                            table[m, a * 128 + (0, 80)[a] + ghost, col] = 1
                        elif 0 <= y < 8 and 0 <= x < 8:
                            table[m, a * 64 + y * 8 + x, col] = 1
                        else:
                            table[m, 128 + 40 * ((m + 1) % 3) + ghost, col] = 1
    return table


def dot(a, b):
    return jnp.dot(a, b, preferred_element_type=F32)


def silu(v):
    return v / (1.0 + jnp.exp(-v))


def lanes_of(shape):
    return lax.broadcasted_iota(jnp.int32, shape, len(shape) - 1)


def splat(flag, shape):
    return jnp.full(shape, jnp.where(flag, 1.0, 0.0).astype(F32), F32)


def pack_taps(raw, packed):
    for dz in range(3):
        packed[dz * 64 : dz * 64 + 64, :] = jnp.concatenate(
            [raw[dz * 9 + t] for t in range(9)], axis=1
        )


def shifted(tile, period):
    lane = lanes_of(tile.shape) % period
    zero = jnp.zeros_like(tile)
    left = jnp.where(lane != 0, pltpu.roll(tile, 1, 1), zero)
    right = jnp.where(lane != period - 1, pltpu.roll(tile, 127, 1), zero)
    return left, tile, right


def stack_rows(tiles, x_ref, start):
    low = lanes_of((64, 128)) < 64
    moved = [shifted(t, 64) for t in tiles]
    for dx in range(3):
        swapped = [pltpu.roll(m[dx], 64, 1) for m in moved]
        for t in range(len(tiles) - 1):
            at = slice(start + t * 128, start + t * 128 + 128)
            x_ref[dx * 64 : dx * 64 + 64, at] = moved[t][dx]
            x_ref[192 + dx * 64 : 256 + dx * 64, at] = jnp.where(low, swapped[t], swapped[t + 1])
            x_ref[384 + dx * 64 : 448 + dx * 64, at] = moved[t + 1][dx]


def kernel(
    fields,
    patch,
    fine,
    w_first,
    w_restrict,
    w_coarse,
    w_prolong,
    w_second,
    w_refine,
    t_split,
    t_spread,
    t_mean,
    t_block,
    base_out,
    fine_out,
    fields_v,
    cells,
    field_t,
    raw_first,
    raw_restrict,
    raw_coarse,
    raw_prolong,
    raw_second,
    raw_refine,
    split_v,
    spread_v,
    mean_v,
    block_v,
    fine_i,
    fine_o,
    k_first,
    k_restrict,
    k_coarse,
    k_prolong,
    k_second,
    k_refine,
    lists,
    live_v,
    pick,
    place,
    x_v,
    y_v,
    act,
    summed,
    coarse_i,
    edge_o,
    edge_i,
    u_v,
    win,
    xf_v,
    load_sem,
    own_sem,
    store_sem,
    s_send,
    s_recv,
    c_send,
    c_recv,
    l_send,
    l_recv,
    f_send,
    f_recv,
    b_send,
    b_recv,
):
    g = lax.axis_index("gz")
    h = lax.axis_index("gx")
    n_g = lax.axis_size("gz")
    n_h = lax.axis_size("gx")

    def near(dz, dy):
        return (lax.rem(g + dz + n_g, n_g), lax.rem(h + dy + n_h, n_h))

    barrier = pltpu.get_barrier_semaphore()
    partners = DIRS + [(0, 2)]
    for dz, dy in partners:
        pl.semaphore_signal(barrier, inc=1, device_id=near(dz, dy), device_id_type=MESH)

    loads = []
    for i, (src, dst) in enumerate(
        [
            (fields, fields_v),
            (w_first, raw_first),
            (w_restrict, raw_restrict),
            (t_split, split_v),
            (w_refine, raw_refine),
            (t_block, block_v),
            (w_coarse, raw_coarse),
            (w_prolong, raw_prolong),
            (w_second, raw_second),
            (t_spread, spread_v),
            (t_mean, mean_v),
        ]
    ):
        loads.append(pltpu.make_async_copy(src, dst, load_sem.at[i]))
    loads[0].start()
    own_fine = pltpu.make_async_copy(
        fine.at[0, pl.ds(2 * h, 2)], fine_i.at[h], own_sem.at[0]
    )

    lists[h] = jnp.zeros((8, 128), jnp.int32)
    lists[h, 0:1, 0:8] = patch[...]

    loads[0].wait()
    for copy in loads[1:] + [own_fine]:
        copy.start()
    cells[...] = fields_v[...].astype(F32).reshape(2048, 64)
    for z in range(4):
        for j in range(4):
            pair = [cells[pl.ds(z * 8 + 2 * j + q, 64, stride=32), :] for q in range(2)]
            field_t[2 + z, 1 + j] = jnp.concatenate(pair, axis=1).astype(BF)

    pl.semaphore_wait(barrier, len(partners))

    def span_of(d, own, width, low, high):
        if d == 0:
            return pl.ds(low, own), pl.ds(low, own)
        if d > 0:
            return pl.ds(low + own - width, width), pl.ds(low - width, width)
        return pl.ds(low, width), pl.ds(high, width)

    sends = {}
    for i, (dz, dy) in enumerate(DIRS):
        zs, zd = span_of(dz, 4, 2, 2, 6)
        ys, yd = span_of(dy, 4, 1, 1, 5)
        sends[dz, dy] = pltpu.make_async_remote_copy(
            src_ref=field_t.at[zs, ys],
            dst_ref=field_t.at[zd, yd],
            send_sem=s_send.at[i],
            recv_sem=s_recv.at[i],
            device_id=near(dz, dy),
            device_id_type=MESH,
        )
    order = [(-1, -1), (-1, 1), (1, -1), (1, 1), (0, -1), (0, 1), (-1, 0), (1, 0)]
    for d in order:
        sends[d].start()
    list_sends = []
    fine_sends = []
    for d in (2, 1, 3):
        peer = near(0, d)
        list_sends.append(
            pltpu.make_async_remote_copy(
                src_ref=lists.at[h],
                dst_ref=lists.at[h],
                send_sem=l_send.at[d - 1],
                recv_sem=l_recv.at[d - 1],
                device_id=peer,
                device_id_type=MESH,
            )
        )
        list_sends[-1].start()
    first_z, last_z = g == 0, g == n_g - 1
    ok_low = splat(h != 0, (64, 128)).astype(BF)
    ok_high = splat(h != n_h - 1, (64, 128)).astype(BF)
    ok_first = splat(g != 0, (64, 128)).astype(BF)
    ok_last = splat(g != n_g - 1, (64, 128)).astype(BF)

    def field(p, t):
        tile = field_t[p, t]
        if t == 0:
            tile = tile * ok_low
        if t == 5:
            tile = tile * ok_high
        if p < 2:
            tile = tile * ok_first
        if p >= 6:
            tile = tile * ok_last
        return tile

    turn = [0]

    def conv_part(load, weight, runs):
        x_ref = x_v.at[turn[0] % 2]
        turn[0] += 1
        start = 0
        for p, first, last in runs:
            stack_rows([load(p, t) for t in range(first, last + 2)], x_ref, start)
            start += (last + 1 - first) * 128
        total = dot(weight[...], x_ref[:, 0:start])
        start = 0
        for p, first, last in runs:
            size = (last + 1 - first) * 128
            y_v[p, :, first * 128 : first * 128 + size] = total[:, start : start + size]
            start += size

    loads[1].wait()
    pack_taps(raw_first, k_first)
    for d in order[:6]:
        sends[d].wait_send()
    for d in (2, 1, 3):
        peer = near(0, d)
        fine_sends.append(
            pltpu.make_async_remote_copy(
                src_ref=fine.at[0, pl.ds(2 * peer[1], 2)],
                dst_ref=fine_i.at[h],
                send_sem=f_send.at[d - 1],
                recv_sem=f_recv.at[d - 1],
                device_id=peer,
                device_id_type=MESH,
            )
        )
        fine_sends[-1].start()

    conv_part(field, k_first, [(2, 1, 3), (3, 1, 3)])
    conv_part(field, k_first, [(4, 1, 3), (5, 1, 3)])

    for copy in loads[2:]:
        copy.wait()
    pack_taps(raw_coarse, k_coarse)
    pack_taps(raw_second, k_second)
    pack_taps(raw_refine, k_refine)
    k_restrict[...] = jnp.concatenate([raw_restrict[t] for t in range(8)], axis=1)
    for p in range(2):
        k_prolong[p * 64 : p * 64 + 64, :] = jnp.concatenate(
            [raw_prolong[p * 4 + t] for t in range(4)], axis=1
        )

    for copy in list_sends:
        copy.wait_recv()
    entry = lax.broadcasted_iota(jnp.int32, (8, 128), 1)
    lane = lanes_of((1, 128)).astype(F32)
    line = jnp.floor((lane + 0.5) * (1.0 / 6.0))
    place_x = lane - 6.0 * line - 1.0
    source = lax.broadcasted_iota(jnp.int32, (640, 128), 0).astype(F32)
    target = lanes_of((64, 512)).astype(F32)
    inner = (lax.broadcasted_iota(jnp.int32, (64, 1), 0) % 16).astype(F32)
    inner_y = jnp.floor(inner * 0.25)
    inner = inner_y * 64.0 + (inner - 4.0 * inner_y)
    for k in range(4):
        ids = lists[k].astype(F32)
        for s in range(2):
            at = k * 2 + s
            value = jnp.sum(
                jnp.where(entry == h * 2 + s, ids, 0.0), axis=1, keepdims=True
            )[0:1]
            py = jnp.floor(value * (1.0 / 16.0))
            px4 = 4.0 * (value - 16.0 * py)
            top = 256.0 * (py - 2.0 * h.astype(F32))
            col = place_x + px4
            want = jnp.where(
                (lane < 36.0) & (col >= 0.0) & (col < 64.0), line * 64.0 + col + top, -1.0
            )
            pick[:, at * 128 : at * 128 + 128] = jnp.where(source == want, 1.0, 0.0).astype(BF)
            want = jnp.where(value >= 0.0, inner + px4 + top, -1.0)
            place[at * 64 : at * 64 + 64, :] = jnp.where(target == want, 1.0, 0.0).astype(BF)
            live_v[k, s : s + 1, :] = jnp.where(
                jnp.broadcast_to(value, (1, 128)) >= 0.0, 1.0, 0.0
            )

    for d in ((0, -1), (0, 1)):
        sends[d].wait_recv()
    conv_part(field, k_first, [(p, t, t) for p in (2, 3, 4, 5) for t in (0, 4)])
    for d in order[:4] + order[6:]:
        sends[d].wait_recv()
    conv_part(field, k_first, [(0, 0, 4), (1, 0, 4)])
    conv_part(field, k_first, [(6, 0, 4), (7, 0, 4)])

    ok_rows = [jnp.ones((64, 128), F32)] * 5
    half = lanes_of((64, 128))
    ok_rows[0] = jnp.where((half < 64) & (h == 0), 0.0, 1.0)
    ok_rows[4] = jnp.where((half >= 64) & (h == n_h - 1), 0.0, 1.0)
    for q in range(6):
        for t in range(5):
            at = slice(t * 128, t * 128 + 128)
            value = silu(y_v[q, 0:64, at] + y_v[q + 1, 64:128, at] + y_v[q + 2, 128:192, at])
            if t in (0, 4):
                value = value * ok_rows[t]
            if q in (0, 5):
                value = value * splat(g != (0 if q == 0 else n_g - 1), (64, 128))
            act[q * 64 : q * 64 + 64, at] = value.astype(BF)

    parted = dot(act[64:320, :], split_v[...]).astype(BF)
    gathered = jnp.concatenate(
        [
            jnp.concatenate(
                [
                    parted[(2 * i + p) * 64 : (2 * i + p) * 64 + 64, f * 128 : f * 128 + 128]
                    for p in range(2)
                    for f in range(4)
                ],
                axis=0,
            )
            for i in range(2)
        ],
        axis=1,
    )
    reduced = dot(k_restrict[...], gathered).astype(BF)
    low = half < 64
    one, two = reduced[:, 0:128], reduced[:, 128:256]
    coarse_i[2] = one
    coarse_i[3] = two
    edge_o[0] = jnp.where(low, one, pltpu.roll(two, 64, 1))
    edge_o[1] = jnp.where(low, pltpu.roll(one, 64, 1), two)
    in_sends = []
    for i, (dz, dy) in enumerate(DIRS):
        if dy == 0:
            src, dst = coarse_i.at[pl.ds(2, 2)], coarse_i.at[pl.ds(2 - 2 * dz, 2)]
        else:
            src, dst = edge_o.at[(1 + dy) // 2], edge_i.at[(1 - dy) // 2, 1 - dz]
        in_sends.append(
            pltpu.make_async_remote_copy(
                src_ref=src,
                dst_ref=dst,
                send_sem=c_send.at[i],
                recv_sem=c_recv.at[i],
                device_id=near(dz, dy),
                device_id_type=MESH,
            )
        )
    for i in (0, 2, 5, 7, 3, 4, 1, 6):
        in_sends[i].start()

    for k in range(4):
        found = dot(act[...], pick[:, k * 256 : k * 256 + 256])
        for s in range(2):
            parts = [found[q * 64 : q * 64 + 64, s * 128 : s * 128 + 128] for q in range(6)]
            for t in range(2):
                tile = (
                    parts[3 * t]
                    + pltpu.roll(parts[3 * t + 1], 40, 1)
                    + pltpu.roll(parts[3 * t + 2], 80, 1)
                )
                at = (k * 2 + s) * 64
                win[t, at : at + 64, :] = tile.astype(BF)

    own_fine.wait()
    for copy in fine_sends:
        copy.wait_recv()
    def spread_blocks(d_first, d_second):
        ks = [near(0, d)[1] for d in (d_first, d_second)]
        sides = [
            jnp.concatenate([win[t, pl.ds(pl.multiple_of(k * 128, 128), 128), :] for k in ks], axis=0)
            for t in range(2)
        ]
        for m in range(5):
            if m < 4:
                left = jnp.concatenate(
                    [
                        fine_i[k, :, :, m * 128 : m * 128 + 128].reshape(128, 128)
                        for k in ks
                    ],
                    axis=0,
                )
                right = sides[(m + 1) // 3]
            else:
                left, right = sides
            spread = dot(jnp.concatenate([left, right], axis=1), block_v[m]).astype(BF)
            for i, d in enumerate((d_first, d_second)):
                for s in range(2):
                    row = i * 128 + s * 64
                    for tap in range(9):
                        xf_v[d * 2 + s, tap * 64 : tap * 64 + 64, m * 128 : m * 128 + 128] = spread[
                            row : row + 64, tap * 128 : tap * 128 + 128
                        ]

    low = lanes_of((64, 128)) < 64
    back_sends = []
    for d in (2, 1, 3, 0):
        if d in (2, 3):
            spread_blocks(d, 1 if d == 2 else 0)
        peer = near(0, d)
        k = peer[1]
        for s in range(2):
            total = dot(k_refine[...], xf_v[d * 2 + s])
            alive = jnp.broadcast_to(live_v[k, s : s + 1, :], (64, 128)) > 0.5
            behind = [total[0:64, m * 128 : m * 128 + 128] for m in range(5)]
            ahead = [total[128:192, m * 128 : m * 128 + 128] for m in range(5)]
            behind_r = [pltpu.roll(v, 64, 1) for v in behind[:4]]
            ahead_r = [pltpu.roll(v, 64, 1) for v in ahead[:4]]
            for m in range(4):
                at = slice(m * 128, m * 128 + 128)
                value = total[64:128, at]
                value += jnp.where(low, behind_r[m - 1] if m > 0 else behind[4], behind_r[m])
                value += jnp.where(low, ahead_r[m], ahead_r[m + 1] if m < 3 else ahead[4])
                value += fine_i[k, s, :, at].astype(F32)
                value = jnp.where(alive, value, 0.0)
                fine_o[k, s, :, at] = value.astype(BF)
        if d == 0:
            continue
        back_sends.append(
            pltpu.make_async_remote_copy(
                src_ref=fine_o.at[k],
                dst_ref=fine_out.at[0, pl.ds(2 * h, 2)],
                send_sem=b_send.at[d - 1],
                recv_sem=b_recv.at[d - 1],
                device_id=peer,
                device_id_type=MESH,
            )
        )
        back_sends[-1].start()
    own_store = pltpu.make_async_copy(
        fine_o.at[h], fine_out.at[0, pl.ds(2 * h, 2)], store_sem.at[0]
    )
    own_store.start()
    means = dot(fine_o[...].reshape(512, 512), mean_v[...])
    back = jnp.concatenate(
        [
            (
                means[k * 128 : k * 128 + 64]
                + pltpu.roll(means[k * 128 + 64 : k * 128 + 128], 64, 1)
            ).astype(BF)
            for k in range(4)
        ],
        axis=1,
    )
    wide = lanes_of((64, 512)) % 64 // 16
    zero = jnp.zeros_like(back)
    ones = jnp.where(lanes_of((16, 512)) % 64 < 16, 1.0, 0.0).astype(BF)
    stacked = jnp.concatenate([jnp.where(wide == z, back, zero) for z in range(4)] + [ones], axis=0)
    placed = dot(stacked, place[...])

    for copy in in_sends:
        copy.wait_recv()
    x_ref = x_v.at[turn[0] % 2]
    turn[0] += 1
    for i in range(6):
        before, mid, after = edge_i[0, i // 2], coarse_i[i], edge_i[1, i // 2]
        if i < 2:
            before, mid, after = before * ok_first, mid * ok_first, after * ok_first
        if i >= 4:
            before, mid, after = before * ok_last, mid * ok_last, after * ok_last
        before, after = before * ok_low, after * ok_high
        mid_r = pltpu.roll(mid, 64, 1)
        around = [
            jnp.where(low, pltpu.roll(before, 64, 1) if i % 2 else before, mid_r),
            jnp.where(
                half < 32, pltpu.roll(before, 32 if i % 2 else 96, 1), pltpu.roll(mid, 32, 1)
            ),
            mid,
            jnp.where(half < 96, pltpu.roll(mid, 96, 1), pltpu.roll(after, 32 if i % 2 else 96, 1)),
            jnp.where(low, mid_r, after if i % 2 else pltpu.roll(after, 64, 1)),
        ]
        for a, tile in enumerate(around):
            for dx, moved in enumerate(shifted(tile, 32)):
                for part, dy in ((0, a), (1, a - 2)):
                    if 0 <= dy < 3:
                        at = slice(i * 256 + part * 128, i * 256 + part * 128 + 128)
                        tap = dy * 3 + dx
                        x_ref[tap * 64 : tap * 64 + 64, at] = moved
    total = dot(k_coarse[...], x_ref[...])
    no_row = jnp.where((half < 32) & (h == 0), 0.0, 1.0)
    no_end = jnp.where((half >= 96) & (h == n_h - 1), 0.0, 1.0)
    rows = []
    for i in range(4):
        parts = []
        for part in range(2):
            at = i * 256 + part * 128
            value = silu(
                total[0:64, at : at + 128]
                + total[64:128, at + 256 : at + 384]
                + total[128:192, at + 512 : at + 640]
            )
            value = value * (no_row if part == 0 else no_end)
            if i in (0, 3):
                value = value * splat(g != (0 if i == 0 else n_g - 1), (64, 128))
            parts.append(value.astype(BF))
        rows += [parts[0]] + [pltpu.roll(parts[0], 128 - 32 * j, 1) for j in range(1, 4)]
        rows += [pltpu.roll(parts[1], 128 - 32 * j, 1) for j in range(2, 4)]
    spread = dot(jnp.concatenate(rows, axis=0), spread_v[...]).astype(BF)
    for i in range(4):
        for t in range(5):
            for f in range(4):
                row = (i * 6 + t + 1 - f // 2) * 64
                at = i * 640 + t * 128
                u_v[f * 64 : f * 64 + 64, at : at + 128] = spread[
                    row : row + 64, f * 128 : f * 128 + 128
                ]
    for i in range(4):
        lifted = dot(k_prolong[...], u_v[:, i * 640 : i * 640 + 640])
        for p in range(2):
            q = 2 * i - 1 + p
            if 0 <= q <= 5:
                at = slice(q * 64, q * 64 + 64)
                summed[at, :] = (
                    act[at, :].astype(F32) + lifted[p * 64 : p * 64 + 64, :]
                ).astype(BF)

    def total_in(q, t):
        return summed[q * 64 : q * 64 + 64, t * 128 : t * 128 + 128]

    for q in (0, 2, 4):
        conv_part(total_in, k_second, [(q, 0, 3), (q + 1, 0, 3)])

    for z in range(4):
        for j in range(4):
            at = slice(j * 128, j * 128 + 128)
            value = y_v[z, 0:64, at] + y_v[z + 1, 64:128, at] + y_v[z + 2, 128:192, at]
            value += field_t[2 + z, 1 + j].astype(F32)
            covered = jnp.broadcast_to(placed[256:257, at], (64, 128)) > 0.5
            value = jnp.where(covered, placed[z * 64 : z * 64 + 64, at], value)
            cells[pl.ds(z * 8 + 2 * j, 64, stride=32), :] = value[:, 0:64]
            cells[pl.ds(z * 8 + 2 * j + 1, 64, stride=32), :] = value[:, 64:128]
    fields_v[...] = cells[...].reshape(64, 4, 8, 64).astype(BF)
    base_store = pltpu.make_async_copy(fields_v, base_out, store_sem.at[1])
    base_store.start()
    for copy in back_sends:
        copy.wait_recv()
    for d in order[6:]:
        sends[d].wait_send()
    for copy in list_sends + fine_sends + in_sends + back_sends:
        copy.wait_send()
    own_store.wait()
    base_store.wait()


def finish(base, fine, base_out, fine_out, base_v, fine_v, in_sems, out_sems):
    loads = []
    stores = []
    for i in range(4):
        parts = [
            (base, base_v, base_out, (pl.ds(16 * i, 16),)),
            (fine, fine_v, fine_out, (pl.ds(0, 1), pl.ds(2 * i, 2))),
        ]
        for j, (src, mid, dst, at) in enumerate(parts):
            loads.append(pltpu.make_async_copy(src.at[at], mid.at[at], in_sems.at[2 * i + j]))
            stores.append(pltpu.make_async_copy(mid.at[at], dst.at[at], out_sems.at[2 * i + j]))
    for copy in loads:
        copy.start()
    for load, store in zip(loads, stores):
        load.wait()
        store.start()
    for copy in stores:
        copy.wait()


def body(
    fields,
    block_patch,
    fine_in,
    conv_first,
    restrict_weight,
    coarse_weight,
    prolong_weight,
    conv_second,
    refine_weight,
):
    any_spec = pl.BlockSpec(memory_space=pl.ANY)
    vmem_spec = pl.BlockSpec(memory_space=pltpu.VMEM)
    dma = pltpu.SemaphoreType.DMA
    v = pltpu.VMEM
    results = pl.pallas_call(
        kernel,
        out_shape=[
            jax.ShapeDtypeStruct(fields.shape, BF),
            jax.ShapeDtypeStruct(fine_in.shape, BF),
        ],
        in_specs=[any_spec, vmem_spec] + [any_spec] * 11,
        out_specs=[any_spec, any_spec],
        scratch_shapes=[
            v((64, 4, 8, 64), BF),
            v((2048, 64), F32),
            v((8, 6, 64, 128), BF),
            v((27, 64, 64), BF),
            v((8, 64, 64), BF),
            v((27, 64, 64), BF),
            v((8, 64, 64), BF),
            v((27, 64, 64), BF),
            v((27, 64, 64), BF),
            v((640, 512), BF),
            v((128, 512), BF),
            v((512, 128), BF),
            v((5, 256, 1152), BF),
            v((4, 2, 64, 512), BF),
            v((4, 2, 64, 512), BF),
            v((192, 576), BF),
            v((64, 512), BF),
            v((192, 576), BF),
            v((128, 256), BF),
            v((192, 576), BF),
            v((192, 576), BF),
            v((4, 8, 128), jnp.int32),
            v((4, 8, 128), F32),
            v((640, 1024), BF),
            v((512, 512), BF),
            v((2, 576, 1536), BF),
            v((8, 192, 640), F32),
            v((384, 640), BF),
            v((384, 640), BF),
            v((6, 64, 128), BF),
            v((2, 64, 128), BF),
            v((2, 3, 64, 128), BF),
            v((256, 2560), BF),
            v((2, 512, 128), BF),
            v((8, 576, 640), BF),
            dma((11,)),
            dma((1,)),
            dma((2,)),
            dma((8,)),
            dma((8,)),
            dma((8,)),
            dma((8,)),
            dma((3,)),
            dma((3,)),
            dma((3,)),
            dma((3,)),
            dma((3,)),
            dma((3,)),
        ],
        compiler_params=pltpu.CompilerParams(
            collective_id=0, has_side_effects=True, vmem_limit_bytes=64 * 1024 * 1024
        ),
        cost_estimate=pl.CostEstimate(flops=8 * 10**9, bytes_accessed=8 * 10**6, transcendentals=0),
    )(
        fields,
        block_patch,
        fine_in,
        conv_first,
        restrict_weight,
        coarse_weight,
        prolong_weight,
        conv_second,
        refine_weight,
        jnp.asarray(split_table(), BF),
        jnp.asarray(spread_table(), BF),
        jnp.asarray(mean_table(), BF),
        jnp.asarray(block_table(), BF),
    )
    return pl.pallas_call(
        finish,
        out_shape=[
            jax.ShapeDtypeStruct(fields.shape, BF),
            jax.ShapeDtypeStruct(fine_in.shape, BF),
        ],
        in_specs=[any_spec, any_spec],
        out_specs=[any_spec, any_spec],
        scratch_shapes=[
            v(fields.shape, BF),
            v(fine_in.shape, BF),
            dma((8,)),
            dma((8,)),
        ],
        compiler_params=pltpu.CompilerParams(vmem_limit_bytes=64 * 1024 * 1024),
    )(*results)


def solution(mesh):
    in_specs = (
        P(None, "gz", "gx", None),
        P("gz", "gx"),
        P("gz", "gx", None, None),
        P(),
        P(),
        P(),
        P(),
        P(),
        P(),
    )
    out_specs = (P(None, "gz", "gx", None), P("gz", "gx", None, None))
    return jax.shard_map(body, mesh=mesh, in_specs=in_specs, out_specs=out_specs, check_vma=False)
```
